512 devices in a mesh: blk: 64 (over z, x, y_lo), head: 8 (over y_hi, core).
Axes of the slice: x: 4, y: 8 (y_hi: 4, y_lo: 2; y = y_hi * 2 + y_lo), z: 8, core: 2. Of those that a mesh axis runs over, the one named last changes fastest.
Arguments:
- queries: bfloat16 [65536, 2048], P('blk', 'head'), parts along dimension 1, may hold values from -6 to 6
- outputs: bfloat16 [65536, 2048], P('blk', 'head'), parts along dimension 1, may hold values from -6 to 6
- out_grads: bfloat16 [65536, 2048], P('blk', 'head'), parts along dimension 1, may hold values from -9 to 9
- log_sums: float32 [32, 65536], P('head', 'blk'), parts along dimension 0, may hold values from 4.5 to 6
- key_values: bfloat16 [65536, 1024], P('blk', 'head'), parts along dimension 1, may hold values from -6 to 6
- holding: int32 [128], replicated, may hold values from 0 to 127, as said below
- block_mask: int32 [128, 3], P('blk'), may hold values 0 or 1
Outputs:
- query_grads: bfloat16 [65536, 2048], P('blk', 'head'), parts along dimension 1
- key_value_grads: bfloat16 [65536, 1024], P('blk', 'head'), parts along dimension 1
The draws below stay inside these ranges and needn't reach their ends.
There are 8 independent parts, one for each index of `head`. The reference program is written for one: setup_inputs(seed, part) draws one part's arguments, and reference() takes and returns one part's arrays. A program takes and returns all parts, laid end to end along the dimension named above; an argument that names none is the same for every part. Nothing has to cross between parts.
Inputs may be any that keep to these rules, and one draw needn't show every extreme that they name: `holding`: A permutation of the 128 blocks. Row block t lies on device t // 2; the block it holds belongs (block // 2) to that device or to the one just before or after it. Two neighbouring devices hold the same number of each other's blocks, at most 1; the first two devices and the last two devices always hold exactly 1 of each other's.
All inputs are finite; a program needn't handle non-finite values. No bound on the sum of `block_mask` on one device may be relied on, other than what follows from the above.
Results may differ from the reference program's by a relative error of at most 0.0049.
Values may be sent and summed in bfloat16 or wider, within the bound.
A program may use at most 64 MiB of HBM per device.

```python
import jax
import jax.numpy as jnp
from jax import lax

HD = 64
QH = 4
BLK_ROWS = 512
BPD = 2
SPAN = 3
NBLOCKS = 128
TOKENS = 65536


def draw_holding(key, part):
    key = jax.random.fold_in(key, 7)
    count_key, forced_key, order_key = jax.random.split(key, 3)
    devices = NBLOCKS // BPD
    spare_slots = BPD // 2
    moved_counts = jax.random.randint(count_key, (devices - 1,), 0, spare_slots + 1)
    forced = jax.random.randint(forced_key, (), 0, devices - 1)
    pair_ids = jnp.arange(devices - 1)
    full_pair = (pair_ids == forced) | (pair_ids == 0) | (pair_ids == devices - 2)
    moved_counts = jnp.where(full_pair, spare_slots, moved_counts).astype(jnp.int32)
    nothing = jnp.zeros((1,), jnp.int32)
    from_prev = jnp.concatenate([nothing, moved_counts])[:, None]
    to_next = jnp.concatenate([moved_counts, nothing])[:, None]
    owner_ids = jnp.arange(devices, dtype=jnp.int32)[:, None]
    slot_ids = jnp.arange(BPD, dtype=jnp.int32)[None, :]
    take_prev = slot_ids < from_prev
    take_next = slot_ids >= BPD - to_next
    source_dev = jnp.where(take_prev, owner_ids - 1, jnp.where(take_next, owner_ids + 1, owner_ids))
    source_slot = jnp.where(take_prev, BPD - from_prev + slot_ids, jnp.where(take_next, slot_ids - (BPD - to_next), slot_ids))
    held_blocks = source_dev * BPD + source_slot
    shuffle = jax.vmap(lambda sub_key: jax.random.permutation(sub_key, BPD))(jax.random.split(order_key, devices))
    held_blocks = jnp.take_along_axis(held_blocks, shuffle.astype(jnp.int32), axis=1)
    return held_blocks.reshape(NBLOCKS).astype(jnp.int32)


def set_ends(result, key, smallest, top_value):
    dims = result.shape
    index_at = [jax.random.randint(jax.random.fold_in(key, axis), (), 0, dims[axis]) for axis in range(len(dims))]
    result = result.at[tuple(index_at)].set(smallest)
    longest = dims.index(max(dims))
    index_at[longest] = (index_at[longest] + 1) % dims[longest]
    return result.at[tuple(index_at)].set(top_value)


def steps_of(own_key, extent, shards, least, largest):
    def one(position, parts):
        heights = jax.random.uniform(jax.random.fold_in(jax.random.fold_in(own_key, 6), position), (parts,), jnp.float32, least / len(shards), largest / len(shards))
        return jnp.repeat(jnp.exp(heights), extent[position] // parts).reshape((-1,) + (1,) * (len(extent) - position - 1))

    loudness = one(*shards[0])
    for cut in shards[1:]:
        loudness = loudness * one(*cut)
    return loudness


def noise(own_key, shape, scale, bound, shards=(), kind=jnp.bfloat16):
    result = scale * jax.random.normal(own_key, shape, jnp.float32)
    if shards:
        result = result * steps_of(own_key, shape, shards, -0.22, 0.18)
    return jnp.clip(result, -bound, bound).astype(kind)


def setup_inputs(seed: int = 0, part: int = 0) -> dict:
    key_list = jax.random.split(jax.random.key(seed), 8)
    part_splits = jax.random.split(jax.random.fold_in(key_list[7], part), 8)
    queries = noise(part_splits[0], (TOKENS, QH * HD), 1.0, 6.0, ((0, 64),))
    outputs = noise(part_splits[1], (TOKENS, QH * HD), 1.0, 6.0, ((0, 64),))
    out_grads = noise(part_splits[2], (TOKENS, QH * HD), 1.5, 9.0, ((0, 64),))
    log_sums = jnp.clip(4.5 + 1.5 * jax.random.uniform(part_splits[3], (QH, TOKENS), jnp.float32) ** steps_of(part_splits[3], (QH, TOKENS), ((1, 64),), -0.2, 0.2), 4.5, 6.0)
    key_values = noise(part_splits[4], (TOKENS, 2 * HD), 1.0, 6.0, ((0, 64),))
    holding = draw_holding(jax.random.fold_in(key_list[7], 71), part)
    block_mask = set_ends((jax.random.randint(key_list[6], (NBLOCKS, SPAN), 0, 3) < 2).astype(jnp.int32), jax.random.fold_in(key_list[6], 1), 0, 1)
    return {"queries": queries, "outputs": outputs, "out_grads": out_grads, "log_sums": log_sums, "key_values": key_values, "holding": holding, "block_mask": block_mask}


def to_sequence(blocked, holding):
    pieces = blocked.reshape(NBLOCKS, BLK_ROWS, blocked.shape[1])
    placed = jnp.zeros_like(pieces).at[holding].set(pieces)
    return placed.reshape(TOKENS, blocked.shape[1])


def reference(queries, outputs, out_grads, log_sums, key_values, holding, block_mask):
    scaling = HD ** -0.5
    seq_queries = to_sequence(queries, holding)
    seq_outputs = to_sequence(outputs, holding)
    seq_grads = to_sequence(out_grads, holding)
    seq_logsums = to_sequence(log_sums.T, holding).T
    product = seq_outputs.astype(jnp.float32) * seq_grads.astype(jnp.float32)
    row_delta = jnp.sum(product.reshape(TOKENS, QH, HD), axis=2).T
    padded = jnp.concatenate([jnp.zeros((BPD * BLK_ROWS, 2 * HD), key_values.dtype), key_values], axis=0)
    window_rows = SPAN * BLK_ROWS

    def one_block(block_id):
        row_start = block_id * BLK_ROWS
        query_heads = lax.dynamic_slice_in_dim(seq_queries, row_start, BLK_ROWS, 0).astype(jnp.float32).reshape(BLK_ROWS, QH, HD)
        grad_heads = lax.dynamic_slice_in_dim(seq_grads, row_start, BLK_ROWS, 0).astype(jnp.float32).reshape(BLK_ROWS, QH, HD)
        lse_rows = lax.dynamic_slice_in_dim(seq_logsums, row_start, BLK_ROWS, 1)
        delta_rows = lax.dynamic_slice_in_dim(row_delta, row_start, BLK_ROWS, 1)
        window = lax.dynamic_slice_in_dim(padded, row_start, window_rows, 0).astype(jnp.float32)
        key_cols = window[:, :HD]
        value_cols = window[:, HD:]
        row_ids = row_start + jnp.arange(BLK_ROWS, dtype=jnp.int32)[:, None]
        col_ids = row_start - BPD * BLK_ROWS + jnp.arange(window_rows, dtype=jnp.int32)[None, :]
        lag_blocks = BPD - jnp.arange(window_rows, dtype=jnp.int32) // BLK_ROWS
        mask_row = lax.dynamic_index_in_dim(block_mask, block_id, 0, keepdims=False)
        alive_cols = mask_row[lag_blocks]
        allowed = (col_ids <= row_ids) & (col_ids >= 0) & (alive_cols[None, :] == 1)
        scores = jnp.einsum("qhd,kd->hqk", query_heads, key_cols) * scaling
        probs = jnp.where(allowed[None], jnp.exp(scores - lse_rows[:, :, None]), jnp.float32(0.0))
        probs_half = probs.astype(jnp.bfloat16)
        prob_grads = jnp.einsum("qhd,kd->hqk", grad_heads, value_cols)
        score_grads = (probs * (prob_grads - delta_rows[:, :, None]) * scaling).astype(jnp.bfloat16)
        query_part = jnp.einsum("hqk,kd->qhd", score_grads.astype(jnp.float32), key_cols)
        query_part = query_part.reshape(BLK_ROWS, QH * HD).astype(jnp.bfloat16)
        key_part = jnp.einsum("hqk,qhd->kd", score_grads.astype(jnp.float32), query_heads)
        value_part = jnp.einsum("hqk,qhd->kd", probs_half.astype(jnp.float32), grad_heads)
        return query_part, jnp.concatenate([key_part, value_part], axis=1)

    query_blocks, window_grads = lax.map(one_block, jnp.arange(NBLOCKS, dtype=jnp.int32))
    query_grads = query_blocks.reshape(TOKENS, QH * HD)
    window_grads = window_grads.reshape(NBLOCKS, SPAN, BLK_ROWS, 2 * HD)
    summed = jnp.zeros((NBLOCKS + BPD, BLK_ROWS, 2 * HD), jnp.float32)
    for lag_index in range(SPAN):
        summed = summed.at[lag_index:lag_index + NBLOCKS].add(window_grads[:, lag_index])
    key_value_grads = summed[BPD:].reshape(TOKENS, 2 * HD).astype(jnp.bfloat16)
    return query_grads, key_value_grads
```

```python
import functools

import jax
import jax.numpy as jnp
from jax import lax
from jax.experimental import pallas as pl
from jax.experimental.pallas import tpu as pltpu
from jax.sharding import PartitionSpec as P

HD = 64
QH = 4
BLK = 512
BPD = 2
SPAN = 3
ROWS = BPD * BLK
HALF = 256
NCH = 4
LOG2E = 1.4426950408889634
SCALE = HD**-0.5
DEAD = 1e30
MESH = pl.DeviceIdType.MESH
F32 = jnp.float32
BF16 = jnp.bfloat16


def nt(a, b):
    return lax.dot_general(a, b, (((1,), (1,)), ((), ())), preferred_element_type=F32)


def nn(a, b):
    return lax.dot_general(a, b, (((1,), (0,)), ((), ())), preferred_element_type=F32)


def pick(cond, a, b):
    return lax.select(jnp.broadcast_to(cond, a.shape), a, b)


def kernel(
    n,
    q_ref, o_ref, do_ref, lse_ref, kv_ref, holding_ref, mask_ref,
    dq_ref, dkv_ref,
    qv, ov, dov, lsev, kvw, ktw, sendb, recvb, stat_send, stat_pool, lsew, deltaw, wbuf,
    acc, dqt, dqo, dkv_send, dkv_in, dkv_out,
    load_sem, out_sem, send_sem, recv_sem,
):
    me = lax.axis_index("blk")
    nxt = lax.rem(me + 1, n)
    prv = lax.rem(me + n - 1, n)

    loads = []
    for p in range(2):
        cols = pl.ds(p * 128, 128)
        loads.append(pltpu.make_async_copy(q_ref.at[:, cols], qv.at[p], load_sem.at[3 * p]))
        loads.append(pltpu.make_async_copy(do_ref.at[:, cols], dov.at[p], load_sem.at[3 * p + 1]))
        loads.append(pltpu.make_async_copy(o_ref.at[:, cols], ov.at[p], load_sem.at[3 * p + 2]))
    load_lse = pltpu.make_async_copy(lse_ref, lsev, load_sem.at[6])
    load_kv = pltpu.make_async_copy(kv_ref, kvw.at[pl.ds(ROWS, ROWS)], load_sem.at[7])
    load_kv.start()
    for c in loads:
        c.start()
    load_lse.start()

    barrier = pltpu.get_barrier_semaphore()
    for dev in (prv, nxt):
        pl.semaphore_signal(barrier, inc=1, device_id={"blk": dev}, device_id_type=MESH)
    pl.semaphore_wait(barrier, 2)

    def remote(src, dst, idx, dev):
        return pltpu.make_async_remote_copy(
            src_ref=src, dst_ref=dst, send_sem=send_sem.at[idx], recv_sem=recv_sem.at[idx],
            device_id={"blk": dev}, device_id_type=MESH,
        )

    kv_copy = remote(kvw.at[pl.ds(ROWS, ROWS)], kvw.at[pl.ds(0, ROWS)], 0, nxt)
    stat_copies = [
        remote(stat_send.at[0], stat_pool.at[2], 1, nxt),
        remote(stat_send.at[1], stat_pool.at[3], 2, prv),
    ]

    def row_copy(j, side):
        return remote(sendb.at[side, j], recvb.at[side, j], 4 + 2 * j + side, nxt if side == 0 else prv)

    dkv_copy = remote(dkv_send, dkv_in, 3, prv)

    load_kv.wait()
    kv_copy.start()

    h0 = holding_ref[2 * me]
    h1 = holding_ref[2 * me + 1]
    p0 = holding_ref[2 * prv]
    p1 = holding_ref[2 * prv + 1]
    second = [(h1 >> 1) == me + 1, (h1 >> 1) == me - 1]
    for c in loads:
        c.wait()
    for j in range(NCH):
        t, p = j // 2, j % 2
        first_rows = pl.ds(t * HALF, HALF)
        second_rows = pl.ds(BLK + t * HALF, HALF)
        for side in range(2):
            for a, src in enumerate((qv, dov)):
                sendb[side, j, a] = pick(second[side], src[p, second_rows, :], src[p, first_rows, :])
            row_copy(j, side).start()

    load_lse.wait()
    head_of = lax.broadcasted_iota(jnp.int32, (8, 128), 1) // HD
    row_of = lax.broadcasted_iota(jnp.int32, (8, 128), 0)
    delta = jnp.zeros((8, ROWS), F32)
    for p in range(2):
        prod = ov[p].astype(F32) * dov[p].astype(F32)
        hi = prod.astype(BF16)
        lo = (prod - hi.astype(F32)).astype(BF16)
        ind = (row_of == head_of + 4 + 2 * p).astype(BF16)
        delta = delta + nt(ind, hi) + nt(ind, lo)
    for slot in range(BPD):
        cols = pl.ds(slot * BLK, BLK)
        stat_pool[slot, 4:8, :] = delta[4:8, slot * BLK : (slot + 1) * BLK]
        stat_pool[slot, 0:4, :] = lsev[:, cols] * LOG2E
    for side in range(2):
        stat_send[side] = pick(second[side], stat_pool[1], stat_pool[0])
        stat_copies[side].start()

    def transpose_keys(base):
        for i in range(ROWS // HALF):
            kt = kvw[pl.ds(base + i * HALF, HALF), :].astype(F32).T
            ktw[base // HALF + i] = kt[:HD].astype(BF16)

    transpose_keys(ROWS)
    acc[...] = jnp.zeros_like(acc)

    for c in stat_copies:
        c.wait_recv()
    is0, is1, isp = [], [], []
    for s in range(BPD):
        b = BPD * me + s
        is0.append(h0 == b)
        is1.append(h1 == b)
        isp.append((p0 == b) | (p1 == b))

    def choose(s, own0, own1, before, after):
        return pick(is0[s], own0, pick(is1[s], own1, pick(isp[s], before, after)))

    for s in range(BPD):
        st = choose(s, stat_pool[0], stat_pool[1], stat_pool[2], stat_pool[3])
        for w in range(SPAN):
            alive = (mask_ref[s, w] == 1) & (BPD * me + s >= w)
            bias = jnp.where(alive, 0.0, DEAD).astype(F32)
            lw = st + bias
            for h in range(QH):
                for t in range(2):
                    lsew[s, w, t, h] = lw[h : h + 1, t * HALF : (t + 1) * HALF]
        for h in range(QH):
            for t in range(2):
                deltaw[s, t, h] = st[4 + h : 5 + h, t * HALF : (t + 1) * HALF]

    kv_copy.wait_recv()
    transpose_keys(0)

    low = lax.broadcasted_iota(jnp.int32, (HALF, 128), 1) < HD
    causal = lax.broadcasted_iota(jnp.int32, (HALF, HALF), 0) <= lax.broadcasted_iota(
        jnp.int32, (HALF, HALF), 1
    )

    def unit(j, s, ct, masked):
        t, p = j // 2, j % 2
        tile = 2 * s + ct
        rows = pl.ds(pl.multiple_of(tile * HALF, HALF), HALF)
        kv = kvw[rows, :]
        kt = ktw[tile]
        w = 2 - ct // 2
        total = acc[rows, :]
        for hp in range(2):
            w1 = wbuf[s, hp, 0]
            w2 = wbuf[s, hp, 1]
            h = 2 * p + hp
            x = nt(kv, w1) * (SCALE * LOG2E) - lsew[s, w, t, h]
            probs = jnp.exp2(x)
            if masked:
                probs = jnp.where(causal, probs, 0.0)
            ds = (probs * (nt(kv, w2) - deltaw[s, t, h])).astype(BF16)
            total = total + nn(ds, w1) + nn(probs.astype(BF16), w2)
            dqt[s, pl.ds(hp * HD, HD), :] += nn(kt, ds)
        acc[rows, :] = total

    def chunk(j, _):
        t, p = j // 2, j % 2
        row_copy(j, 0).wait_recv()
        row_copy(j, 1).wait_recv()
        for s in range(BPD):
            rows0 = pl.ds(pl.multiple_of(t * HALF, HALF), HALF)
            rows1 = pl.ds(pl.multiple_of(BLK + t * HALF, HALF), HALF)
            qs = choose(s, qv[p, rows0, :], qv[p, rows1, :], recvb[0, j, 0], recvb[1, j, 0]).astype(F32)
            ds = choose(s, dov[p, rows0, :], dov[p, rows1, :], recvb[0, j, 1], recvb[1, j, 1]).astype(F32)
            wbuf[s, 0, 0] = jnp.where(low, qs, 0.0).astype(BF16)
            wbuf[s, 1, 0] = jnp.where(low, pltpu.roll(qs, HD, 1), 0.0).astype(BF16)
            wbuf[s, 0, 1] = jnp.where(low, 0.0, pltpu.roll(ds, HD, 1)).astype(BF16)
            wbuf[s, 1, 1] = jnp.where(low, 0.0, ds).astype(BF16)
        dqt[...] = jnp.zeros_like(dqt)

        def run(s, lo, hi):
            lax.fori_loop(lo, hi, lambda ct, _: (unit(j, s, ct, False), 0)[1], 0)

        run(0, 0, 4)
        run(1, 0, 2)

        @pl.when(j == NCH - 1)
        def _():
            scaled = jnp.where(low[:1], SCALE, 1.0)
            for i in range(ROWS // HALF):
                r = pl.ds(i * HALF, HALF)
                dkv_send[r, :] = (acc[r, :] * scaled).astype(BF16)
            dkv_copy.start()

        run(0, 4, 4 + t)
        unit(j, 0, 4 + t, True)
        run(1, 2, 4 + t)
        unit(j, 1, 4 + t, True)
        for s in range(BPD):
            dqo[j, s] = (dqt[s].T * SCALE).astype(BF16)
        return 0

    lax.fori_loop(0, NCH, chunk, 0)

    dq_copies = []
    for j in range(NCH):
        t, p = j // 2, j % 2
        for s in range(BPD):
            dst = dq_ref.at[pl.ds(s * BLK + t * HALF, HALF), pl.ds(p * 128, 128)]
            c = pltpu.make_async_copy(dqo.at[j, s], dst, out_sem.at[2 * j + s])
            c.start()
            dq_copies.append(c)

    dkv_copy.wait_recv()
    scaled = jnp.where(low[:1], SCALE, 1.0)
    for i in range(ROWS // HALF):
        r = pl.ds(i * HALF, HALF)
        own = acc[pl.ds(ROWS + i * HALF, HALF), :] * scaled
        dkv_out[r, :] = (own + dkv_in[r, :].astype(F32)).astype(BF16)
    dkv_store = pltpu.make_async_copy(dkv_out, dkv_ref, out_sem.at[8])
    dkv_store.start()

    kv_copy.wait_send()
    for c in stat_copies:
        c.wait_send()
    for j in range(NCH):
        for side in range(2):
            row_copy(j, side).wait_send()
    dkv_copy.wait_send()
    for c in dq_copies:
        c.wait()
    dkv_store.wait()


def on_device(n, queries, outputs, out_grads, log_sums, key_values, holding, block_mask):
    hbm = pl.BlockSpec(memory_space=pl.ANY)
    smem = pl.BlockSpec(memory_space=pltpu.SMEM)
    vm = pltpu.VMEM
    return pl.pallas_call(
        functools.partial(kernel, n),
        out_shape=(
            jax.ShapeDtypeStruct((ROWS, QH * HD), BF16),
            jax.ShapeDtypeStruct((ROWS, 2 * HD), BF16),
        ),
        in_specs=[hbm] * 5 + [smem] * 2,
        out_specs=(hbm, hbm),
        scratch_shapes=[
            vm((2, ROWS, 128), BF16),
            vm((2, ROWS, 128), BF16),
            vm((2, ROWS, 128), BF16),
            vm((QH, ROWS), F32),
            vm((2 * ROWS, 128), BF16),
            vm((2 * ROWS // HALF, HD, HALF), BF16),
            vm((2, NCH, 2, HALF, 128), BF16),
            vm((2, NCH, 2, HALF, 128), BF16),
            vm((2, 8, BLK), F32),
            vm((4, 8, BLK), F32),
            vm((BPD, SPAN, 2, QH, 1, HALF), F32),
            vm((BPD, 2, QH, 1, HALF), F32),
            vm((BPD, 2, 2, HALF, 128), BF16),
            vm((2 * ROWS, 128), F32),
            vm((BPD, 128, HALF), F32),
            vm((NCH, BPD, HALF, 128), BF16),
            vm((ROWS, 128), BF16),
            vm((ROWS, 128), BF16),
            vm((ROWS, 128), BF16),
            pltpu.SemaphoreType.DMA((8,)),
            pltpu.SemaphoreType.DMA((9,)),
            pltpu.SemaphoreType.DMA((12,)),
            pltpu.SemaphoreType.DMA((12,)),
        ],
        compiler_params=pltpu.CompilerParams(
            collective_id=0, has_side_effects=True, vmem_limit_bytes=40 * 1024 * 1024
        ),
    )(queries, outputs, out_grads, log_sums, key_values, holding, block_mask)


def solution(mesh):
    in_specs = (
        P("blk", "head"),
        P("blk", "head"),
        P("blk", "head"),
        P("head", "blk"),
        P("blk", "head"),
        P(),
        P("blk", None),
    )
    out_specs = (P("blk", "head"), P("blk", "head"))
    return jax.shard_map(
        functools.partial(on_device, mesh.shape["blk"]),
        mesh=mesh, in_specs=in_specs, out_specs=out_specs, check_vma=False,
    )
```

```python
import functools

import jax
import jax.numpy as jnp
from jax import lax
from jax.experimental import pallas as pl
from jax.experimental.pallas import tpu as pltpu
from jax.sharding import PartitionSpec as P

HD = 64
QH = 4
BLK = 512
BPD = 2
SPAN = 3
ROWS = BPD * BLK
HALF = 256
NCH = 8
LOG2E = 1.4426950408889634
SCALE = HD**-0.5
DEAD = 1e30
MESH = pl.DeviceIdType.MESH
F32 = jnp.float32
BF16 = jnp.bfloat16


def nt(a, b):
    return lax.dot_general(a, b, (((1,), (1,)), ((), ())), preferred_element_type=F32)


def nn(a, b):
    return lax.dot_general(a, b, (((1,), (0,)), ((), ())), preferred_element_type=F32)


def pick(cond, a, b):
    return lax.select(jnp.broadcast_to(cond, a.shape), a, b)


def kernel(
    n,
    q_ref, o_ref, do_ref, lse_ref, kv_ref, holding_ref, mask_ref,
    dq_ref, dkv_ref,
    qv, ov, dov, lsev, kvw, ktw, packed, sendb, recvb, stat_send, stat_pool, lsew, deltaw, wbuf,
    acc, dqt, dqo, dkv_send, dkv_in, dkv_out,
    load_sem, out_sem, send_sem, recv_sem,
):
    me = lax.axis_index("blk")
    nxt = lax.rem(me + 1, n)
    prv = lax.rem(me + n - 1, n)

    barrier = pltpu.get_barrier_semaphore()
    for dev in (prv, nxt):
        pl.semaphore_signal(barrier, inc=1, device_id={"blk": dev}, device_id_type=MESH)

    loads, load_outs = [], []
    for p in range(2):
        cols = pl.ds(p * 128, 128)
        loads.append(pltpu.make_async_copy(q_ref.at[:, cols], qv.at[p], load_sem.at[3 * p]))
        loads.append(pltpu.make_async_copy(do_ref.at[:, cols], dov.at[p], load_sem.at[3 * p + 1]))
        load_outs.append(pltpu.make_async_copy(o_ref.at[:, cols], ov.at[p], load_sem.at[3 * p + 2]))
    load_lse = pltpu.make_async_copy(lse_ref, lsev, load_sem.at[6])
    load_kv = pltpu.make_async_copy(kv_ref, kvw.at[pl.ds(ROWS, ROWS)], load_sem.at[7])
    for c in loads:
        c.start()
    load_kv.start()
    load_lse.start()
    for c in load_outs:
        c.start()

    def remote(src, dst, idx, dev):
        return pltpu.make_async_remote_copy(
            src_ref=src, dst_ref=dst, send_sem=send_sem.at[idx], recv_sem=recv_sem.at[idx],
            device_id={"blk": dev}, device_id_type=MESH,
        )

    kv_copy = remote(kvw.at[pl.ds(ROWS, ROWS)], kvw.at[pl.ds(0, ROWS)], 0, nxt)
    stat_copies = [
        remote(stat_send.at[0], stat_pool.at[2], 1, nxt),
        remote(stat_send.at[1], stat_pool.at[3], 2, prv),
    ]
    dkv_copies = [
        remote(dkv_send.at[pl.ds(i * BLK, BLK)], dkv_in.at[pl.ds(i * BLK, BLK)], 3 + i, prv)
        for i in range(BPD)
    ]

    def row_copy(j, side):
        return remote(sendb.at[side, j], recvb.at[side, j], 5 + 2 * j + side, nxt if side == 0 else prv)

    h0 = holding_ref[2 * me]
    h1 = holding_ref[2 * me + 1]
    p0 = holding_ref[2 * prv]
    p1 = holding_ref[2 * prv + 1]
    second = [(h1 >> 1) == me + 1, (h1 >> 1) == me - 1]
    low = lax.broadcasted_iota(jnp.int32, (HALF, 128), 1) < HD

    def pack(t, p):
        for slot in range(BPD):
            r = pl.ds(slot * BLK + t * HALF, HALF)
            qf = qv[p, r, :].astype(F32)
            df = dov[p, r, :].astype(F32)
            j = 4 * (1 - t) + 2 * p
            packed[slot, j] = jnp.where(low, qf, pltpu.roll(df, HD, 1)).astype(BF16)
            packed[slot, j + 1] = jnp.where(low, pltpu.roll(qf, HD, 1), df).astype(BF16)
        for j in (j, j + 1):
            for side in range(2):
                sendb[side, j] = pick(second[side], packed[1, j], packed[0, j])

    for c in loads[:2]:
        c.wait()
    pack(1, 0)
    pl.semaphore_wait(barrier, 2)
    for j in range(2):
        for side in range(2):
            row_copy(j, side).start()
    load_kv.wait()
    kv_copy.start()

    for c in loads[2:]:
        c.wait()
    load_lse.wait()
    for c in load_outs:
        c.wait()
    head_of = lax.broadcasted_iota(jnp.int32, (8, 128), 1) // HD
    row_of = lax.broadcasted_iota(jnp.int32, (8, 128), 0)
    delta = jnp.zeros((8, ROWS), F32)
    for p in range(2):
        prod = ov[p].astype(F32) * dov[p].astype(F32)
        hi = prod.astype(BF16)
        lo = (prod - hi.astype(F32)).astype(BF16)
        ind = (row_of == head_of + 4 + 2 * p).astype(BF16)
        delta = delta + nt(ind, hi) + nt(ind, lo)
    for slot in range(BPD):
        cols = pl.ds(slot * BLK, BLK)
        stat_pool[slot, 4:8, :] = delta[4:8, slot * BLK : (slot + 1) * BLK]
        stat_pool[slot, 0:4, :] = lsev[:, cols] * LOG2E
    for side in range(2):
        stat_send[side] = pick(second[side], stat_pool[1], stat_pool[0])
        stat_copies[side].start()

    pack(1, 1)
    pack(0, 0)
    pack(0, 1)

    def transpose_keys(base):
        for i in range(ROWS // HALF):
            kt = kvw[pl.ds(base + i * HALF, HALF), :].astype(F32).T
            ktw[:, pl.ds(base + i * HALF, HALF)] = kt[:HD].astype(BF16)

    transpose_keys(ROWS)
    acc[...] = jnp.zeros_like(acc)

    for c in stat_copies:
        c.wait_recv()
    is0, is1, isp = [], [], []
    for s in range(BPD):
        b = BPD * me + s
        is0.append(h0 == b)
        is1.append(h1 == b)
        isp.append((p0 == b) | (p1 == b))

    def choose(s, own0, own1, before, after):
        return pick(is0[s], own0, pick(is1[s], own1, pick(isp[s], before, after)))

    for s in range(BPD):
        st = choose(s, stat_pool[0], stat_pool[1], stat_pool[2], stat_pool[3])
        for w in range(SPAN):
            alive = (mask_ref[s, w] == 1) & (BPD * me + s >= w)
            bias = jnp.where(alive, 0.0, DEAD).astype(F32)
            lw = st + bias
            for h in range(QH):
                for t in range(2):
                    lsew[s, w, t, h] = lw[h : h + 1, t * HALF : (t + 1) * HALF]
        for h in range(QH):
            for t in range(2):
                deltaw[s, t, h] = st[4 + h : 5 + h, t * HALF : (t + 1) * HALF]

    kv_copy.wait_recv()
    transpose_keys(0)

    causal = lax.broadcasted_iota(jnp.int32, (HALF, HALF), 0) <= lax.broadcasted_iota(
        jnp.int32, (HALF, HALF), 1
    )
    low_half = low[:1].astype(BF16)
    high_half = (~low[:1]).astype(BF16)

    def attend(t, h, s, base, segments, first):
        size = sum(seg[0] for seg in segments)
        rows = pl.ds(base, size)
        j = 4 * (1 - t) + h
        w1 = wbuf[j, s, 0]
        w2 = wbuf[j, s, 1]
        kv = kvw[rows, :]
        scores = nt(kv, w1)
        prob_grads = nt(kv, w2)
        dlt = deltaw[s, t, h]
        probs, grads = [], []
        at = 0
        for count, w, masked in segments:
            pr = jnp.exp2(scores[at : at + count] * (SCALE * LOG2E) - lsew[s, w, t, h])
            if masked:
                pr = jnp.where(causal, pr, 0.0)
            probs.append(pr.astype(BF16))
            grads.append((pr * (prob_grads[at : at + count] - dlt)).astype(BF16))
            at += count
        pb = jnp.concatenate(probs, axis=0) if len(probs) > 1 else probs[0]
        gb = jnp.concatenate(grads, axis=0) if len(grads) > 1 else grads[0]
        acc[rows, :] += nn(gb, w1) + nn(pb, w2)
        part = nn(ktw[:, rows], gb)
        cols = pl.ds(pl.multiple_of(h * HD, HD), HD)
        if first:
            dqt[t, s, cols, :] = part
        else:
            dqt[t, s, cols, :] += part

    def prior(t, h):
        attend(t, h, 0, 0, [(BLK, 2, False), (BLK, 1, False)], True)
        attend(t, h, 1, BLK, [(BLK, 2, False)], True)

    def own(t, h):
        diagonal = [(HALF, 0, False)] * t + [(HALF, 0, True)]
        attend(t, h, 0, ROWS, diagonal, False)
        attend(t, h, 1, ROWS, [(BLK, 1, False)] + diagonal, False)

    def arrive(j):
        row_copy(j, 0).wait_recv()
        row_copy(j, 1).wait_recv()

    def weights(j):
        for s in range(BPD):
            x = choose(s, packed[0, j], packed[1, j], recvb[0, j], recvb[1, j])
            wbuf[j, s, 0] = x * low_half
            wbuf[j, s, 1] = x * high_half

    def send_rows(j):
        row_copy(j, 0).start()
        row_copy(j, 1).start()

    def store_queries(t):
        copies = []
        for s in range(BPD):
            r = pl.ds(s * BLK + t * HALF, HALF)
            dqo[r, :] = (dqt[t, s].T * SCALE).astype(BF16)
            c = pltpu.make_async_copy(dqo.at[r], dq_ref.at[r], out_sem.at[2 * t + s])
            c.start()
            copies.append(c)
        return copies

    def later_rows(h, _):
        arrive(h)
        send_rows(h + 2)
        weights(h)
        prior(1, h)
        own(1, h)
        return 0

    lax.fori_loop(0, QH, later_rows, 0)

    def earlier_rows(h, _):
        j = h + QH
        arrive(j)

        @pl.when(j + 2 < NCH)
        def _():
            send_rows(j + 2)

        weights(j)
        prior(0, h)
        return 0

    lax.fori_loop(0, QH, earlier_rows, 0)

    scaled = jnp.where(low[:1], SCALE, 1.0)
    for i in range(BPD):
        r = pl.ds(i * BLK, BLK)
        dkv_send[r, :] = (acc[r, :] * scaled).astype(BF16)
        dkv_copies[i].start()

    stores = store_queries(1)

    def earlier_own(h, _):
        own(0, h)
        return 0

    lax.fori_loop(0, QH, earlier_own, 0)
    stores += store_queries(0)

    for i in range(BPD):
        r = pl.ds(i * BLK, BLK)
        dkv_copies[i].wait_recv()
        mine = acc[pl.ds(ROWS + i * BLK, BLK), :] * scaled
        dkv_out[r, :] = (mine + dkv_in[r, :].astype(F32)).astype(BF16)
        c = pltpu.make_async_copy(dkv_out.at[r], dkv_ref.at[r], out_sem.at[4 + i])
        c.start()
        stores.append(c)

    kv_copy.wait_send()
    for c in stat_copies:
        c.wait_send()
    for j in range(NCH):
        for side in range(2):
            row_copy(j, side).wait_send()
    for c in dkv_copies:
        c.wait_send()
    for c in stores:
        c.wait()


def on_device(n, queries, outputs, out_grads, log_sums, key_values, holding, block_mask):
    hbm = pl.BlockSpec(memory_space=pl.ANY)
    smem = pl.BlockSpec(memory_space=pltpu.SMEM)
    vm = pltpu.VMEM
    return pl.pallas_call(
        functools.partial(kernel, n),
        out_shape=(
            jax.ShapeDtypeStruct((ROWS, QH * HD), BF16),
            jax.ShapeDtypeStruct((ROWS, 2 * HD), BF16),
        ),
        in_specs=[hbm] * 5 + [smem] * 2,
        out_specs=(hbm, hbm),
        scratch_shapes=[
            vm((2, ROWS, 128), BF16),
            vm((2, ROWS, 128), BF16),
            vm((2, ROWS, 128), BF16),
            vm((QH, ROWS), F32),
            vm((2 * ROWS, 128), BF16),
            vm((HD, 2 * ROWS), BF16),
            vm((BPD, NCH, HALF, 128), BF16),
            vm((2, NCH, HALF, 128), BF16),
            vm((2, NCH, HALF, 128), BF16),
            vm((2, 8, BLK), F32),
            vm((4, 8, BLK), F32),
            vm((BPD, SPAN, 2, QH, 1, HALF), F32),
            vm((BPD, 2, QH, 1, HALF), F32),
            vm((NCH, BPD, 2, HALF, 128), BF16),
            vm((2 * ROWS, 128), F32),
            vm((2, BPD, QH * HD, HALF), F32),
            vm((ROWS, QH * HD), BF16),
            vm((ROWS, 128), BF16),
            vm((ROWS, 128), BF16),
            vm((ROWS, 128), BF16),
            pltpu.SemaphoreType.DMA((8,)),
            pltpu.SemaphoreType.DMA((6,)),
            pltpu.SemaphoreType.DMA((21,)),
            pltpu.SemaphoreType.DMA((21,)),
        ],
        compiler_params=pltpu.CompilerParams(
            collective_id=0, has_side_effects=True, vmem_limit_bytes=60 * 1024 * 1024
        ),
    )(queries, outputs, out_grads, log_sums, key_values, holding, block_mask)


def solution(mesh):
    in_specs = (
        P("blk", "head"),
        P("blk", "head"),
        P("blk", "head"),
        P("head", "blk"),
        P("blk", "head"),
        P(),
        P("blk", None),
    )
    out_specs = (P("blk", "head"), P("blk", "head"))
    return jax.shard_map(
        functools.partial(on_device, mesh.shape["blk"]),
        mesh=mesh, in_specs=in_specs, out_specs=out_specs, check_vma=False,
    )
```

```python
import functools

import jax
import jax.numpy as jnp
from jax import lax
from jax.experimental import pallas as pl
from jax.experimental.pallas import tpu as pltpu
from jax.sharding import PartitionSpec as P

HD = 64
QH = 4
BLK = 512
BPD = 2
SPAN = 3
ROWS = BPD * BLK
HALF = 256
NCH = 8
PARTS = 2
LOG2E = 1.4426950408889634
SCALE = HD**-0.5
DEAD = 1e30
MESH = pl.DeviceIdType.MESH
F32 = jnp.float32
BF16 = jnp.bfloat16


def nt(a, b):
    return lax.dot_general(a, b, (((1,), (1,)), ((), ())), preferred_element_type=F32)


def nn(a, b):
    return lax.dot_general(a, b, (((1,), (0,)), ((), ())), preferred_element_type=F32)


def pick(cond, a, b):
    return lax.select(jnp.broadcast_to(cond, a.shape), a, b)


class Copy:
    def __init__(self, src, dst, sent, landed, to_next, nxt, prv, has_nxt, has_prv):
        self.args = dict(
            src_ref=src, dst_ref=dst, send_sem=sent, recv_sem=landed,
            device_id={"blk": nxt if to_next else prv}, device_id_type=MESH,
        )
        self.sends, self.receives = (has_nxt, has_prv) if to_next else (has_prv, has_nxt)

    def start(self):
        pl.when(self.sends)(lambda: pltpu.make_async_remote_copy(**self.args).start())

    def wait_send(self):
        pl.when(self.sends)(lambda: pltpu.make_async_remote_copy(**self.args).wait_send())

    def wait_recv(self):
        pl.when(self.receives)(lambda: pltpu.make_async_remote_copy(**self.args).wait_recv())


def kernel(
    n,
    q_ref, o_ref, do_ref, lse_ref, kv_ref, holding_ref, mask_ref,
    dq_ref, dkv_ref,
    qv, ov, dov, lsev, kvw, ktw, packed, sendb, recvb, stat_send, stat_pool, lsew, deltaw, wbuf,
    acc, dqt, dqo, dkv_send, dkv_in, dkv_out,
    load_sem, out_sem, send_sem, recv_sem,
):
    me = lax.axis_index("blk")
    nxt = lax.rem(me + 1, n)
    prv = lax.rem(me + n - 1, n)

    has_prv = me > 0
    has_nxt = me < n - 1
    barrier = pltpu.get_barrier_semaphore()

    @pl.when(has_prv)
    def _():
        pl.semaphore_signal(barrier, inc=1, device_id={"blk": prv}, device_id_type=MESH)

    @pl.when(has_nxt)
    def _():
        pl.semaphore_signal(barrier, inc=1, device_id={"blk": nxt}, device_id_type=MESH)

    loads, load_outs = [], []
    for p in range(2):
        cols = pl.ds(p * 128, 128)
        loads.append(pltpu.make_async_copy(q_ref.at[:, cols], qv.at[p], load_sem.at[3 * p]))
        loads.append(pltpu.make_async_copy(do_ref.at[:, cols], dov.at[p], load_sem.at[3 * p + 1]))
        load_outs.append(pltpu.make_async_copy(o_ref.at[:, cols], ov.at[p], load_sem.at[3 * p + 2]))
    load_lse = pltpu.make_async_copy(lse_ref, lsev, load_sem.at[6])
    load_kv = pltpu.make_async_copy(kv_ref, kvw.at[pl.ds(ROWS, ROWS)], load_sem.at[7])
    for c in loads:
        c.start()
    load_kv.start()
    load_lse.start()
    for c in load_outs:
        c.start()

    def remote(src, dst, idx, to_next):
        return Copy(src, dst, send_sem.at[idx], recv_sem.at[idx], to_next, nxt, prv, has_nxt, has_prv)

    kv_copy = remote(kv_ref, kvw.at[pl.ds(0, ROWS)], 0, True)
    stat_copies = [
        remote(stat_send.at[0], stat_pool.at[2], 1, True),
        remote(stat_send.at[1], stat_pool.at[3], 2, False),
    ]
    dkv_copies = [
        remote(dkv_send.at[pl.ds(i * BLK, BLK)], dkv_in.at[pl.ds(i * BLK, BLK)], 3 + i, False)
        for i in range(BPD)
    ]

    def row_copy(j, side):
        return remote(sendb.at[side, j], recvb.at[side, j], 5 + 2 * j + side, side == 0)

    h0 = holding_ref[2 * me]
    h1 = holding_ref[2 * me + 1]
    p0 = holding_ref[2 * prv]
    p1 = holding_ref[2 * prv + 1]
    second = [(h1 >> 1) == me + 1, (h1 >> 1) == me - 1]
    low = lax.broadcasted_iota(jnp.int32, (HALF, 128), 1) < HD

    def send_rows(j):
        row_copy(j, 0).start()
        row_copy(j, 1).start()

    def pack(t, p):
        for slot in range(BPD):
            r = pl.ds(slot * BLK + t * HALF, HALF)
            qf = qv[p, r, :].astype(F32)
            df = dov[p, r, :].astype(F32)
            j = 4 * (1 - t) + 2 * p
            packed[slot, j] = jnp.where(low, qf, pltpu.roll(df, HD, 1)).astype(BF16)
            packed[slot, j + 1] = jnp.where(low, pltpu.roll(qf, HD, 1), df).astype(BF16)
        for j in (j, j + 1):
            for side in range(2):
                sendb[side, j] = pick(second[side], packed[1, j], packed[0, j])


    pl.semaphore_wait(barrier, has_prv.astype(jnp.int32) + has_nxt.astype(jnp.int32))

    kv_copy.start()
    for c in loads[:2]:
        c.wait()
    pack(1, 0)
    for j in range(2):
        for side in range(2):
            row_copy(j, side).start()
    load_kv.wait()

    for c in loads[2:]:
        c.wait()
    load_lse.wait()
    for c in load_outs:
        c.wait()
    head_of = lax.broadcasted_iota(jnp.int32, (8, 128), 1) // HD
    row_of = lax.broadcasted_iota(jnp.int32, (8, 128), 0)
    delta = jnp.zeros((8, ROWS), F32)
    for p in range(2):
        prod = ov[p].astype(F32) * dov[p].astype(F32)
        hi = prod.astype(BF16)
        lo = (prod - hi.astype(F32)).astype(BF16)
        ind = (row_of == head_of + 4 + 2 * p).astype(BF16)
        delta = delta + nt(ind, hi) + nt(ind, lo)
    for slot in range(BPD):
        cols = pl.ds(slot * BLK, BLK)
        stat_pool[slot, 4:8, :] = delta[4:8, slot * BLK : (slot + 1) * BLK]
        stat_pool[slot, 0:4, :] = lsev[:, cols] * LOG2E
    for side in range(2):
        stat_send[side] = pick(second[side], stat_pool[1], stat_pool[0])
        stat_copies[side].start()

    pack(1, 1)
    send_rows(2)
    pack(0, 0)
    pack(0, 1)

    def transpose_keys(base):
        for i in range(ROWS // HALF):
            kt = kvw[pl.ds(base + i * HALF, HALF), :].astype(F32).T
            ktw[:, pl.ds(base + i * HALF, HALF)] = kt[:HD].astype(BF16)

    transpose_keys(ROWS)
    acc[...] = jnp.zeros_like(acc)

    for c in stat_copies:
        c.wait_recv()
    is0, is1, isp = [], [], []
    for s in range(BPD):
        b = BPD * me + s
        is0.append(h0 == b)
        is1.append(h1 == b)
        isp.append((p0 == b) | (p1 == b))

    def choose(s, own0, own1, before, after):
        return pick(is0[s], own0, pick(is1[s], own1, pick(isp[s], before, after)))

    for s in range(BPD):
        st = choose(s, stat_pool[0], stat_pool[1], stat_pool[2], stat_pool[3])
        for w in range(SPAN):
            alive = (mask_ref[s, w] == 1) & (BPD * me + s >= w)
            bias = jnp.where(alive, 0.0, DEAD).astype(F32)
            lw = st + bias
            for h in range(QH):
                for t in range(2):
                    lsew[s, w, t, h] = lw[h : h + 1, t * HALF : (t + 1) * HALF]
        for h in range(QH):
            for t in range(2):
                deltaw[s, t, h] = st[4 + h : 5 + h, t * HALF : (t + 1) * HALF]

    kv_copy.wait_recv()

    @pl.when(me == 0)
    def _():
        kvw[pl.ds(0, ROWS), :] = jnp.zeros((ROWS, 128), BF16)

    @pl.when(me == n - 1)
    def _():
        dkv_in[...] = jnp.zeros_like(dkv_in)

    transpose_keys(0)

    causal = lax.broadcasted_iota(jnp.int32, (HALF, HALF), 0) <= lax.broadcasted_iota(
        jnp.int32, (HALF, HALF), 1
    )
    low_half = low[:1].astype(BF16)
    high_half = (~low[:1]).astype(BF16)

    def attend(t, h, s, base, segments, first):
        size = sum(seg[0] for seg in segments)
        rows = pl.ds(base, size)
        j = 4 * (1 - t) + h
        w1 = wbuf[j, s, 0]
        w2 = wbuf[j, s, 1]
        kv = kvw[rows, :]
        scores = nt(kv, w1)
        prob_grads = nt(kv, w2)
        dlt = deltaw[s, t, h]
        probs, grads = [], []
        at = 0
        for count, w, masked in segments:
            pr = jnp.exp2(scores[at : at + count] * (SCALE * LOG2E) - lsew[s, w, t, h])
            if masked:
                pr = jnp.where(causal, pr, 0.0)
            probs.append(pr.astype(BF16))
            grads.append((pr * (prob_grads[at : at + count] - dlt)).astype(BF16))
            at += count
        pb = jnp.concatenate(probs, axis=0) if len(probs) > 1 else probs[0]
        gb = jnp.concatenate(grads, axis=0) if len(grads) > 1 else grads[0]
        acc[rows, :] += nn(gb, w1) + nn(pb, w2)
        part = nn(ktw[:, rows], gb)
        cols = pl.ds(h * HD if isinstance(h, int) else pl.multiple_of(h * HD, HD), HD)
        if first:
            dqt[t, s, cols, :] = part
        else:
            dqt[t, s, cols, :] += part

    def prior(t, h):
        attend(t, h, 0, 0, [(BLK, 2, False), (BLK, 1, False)], True)
        attend(t, h, 1, BLK, [(BLK, 2, False)], True)

    def own(t, h):
        diagonal = [(HALF, 0, False)] * t + [(HALF, 0, True)]
        attend(t, h, 0, ROWS, diagonal, False)
        attend(t, h, 1, ROWS, [(BLK, 1, False)] + diagonal, False)

    def arrive(j):
        row_copy(j, 0).wait_recv()
        row_copy(j, 1).wait_recv()

    def weights(j):
        for s in range(BPD):
            x = choose(s, packed[0, j], packed[1, j], recvb[0, j], recvb[1, j])
            wbuf[j, s, 0] = x * low_half
            wbuf[j, s, 1] = x * high_half

    def send_rows(j):
        row_copy(j, 0).start()
        row_copy(j, 1).start()

    def store_queries(t):
        copies = []
        for s in range(BPD):
            r = pl.ds(s * BLK + t * HALF, HALF)
            dqo[r, :] = (dqt[t, s].T * SCALE).astype(BF16)
            c = pltpu.make_async_copy(dqo.at[r], dq_ref.at[r], out_sem.at[2 * t + s])
            c.start()
            copies.append(c)
        return copies

    def later_rows(h, _):
        arrive(h)
        send_rows(h + 3)
        weights(h)
        prior(1, h)
        own(1, h)
        return 0

    lax.fori_loop(0, QH, later_rows, 0)

    def earlier_rows(h, _):
        j = h + QH
        arrive(j)

        @pl.when(j + 3 < NCH)
        def _():
            send_rows(j + 3)

        weights(j)
        prior(0, h)
        return 0

    lax.fori_loop(0, QH - 1, earlier_rows, 0)
    arrive(NCH - 1)
    weights(NCH - 1)
    scaled = jnp.where(low[:1], SCALE, 1.0)

    def return_keys(i):
        r = pl.ds(i * BLK, BLK)
        dkv_send[r, :] = (acc[r, :] * scaled).astype(BF16)
        dkv_copies[i].start()

    attend(0, QH - 1, 0, 0, [(BLK, 2, False)], True)
    return_keys(0)
    attend(0, QH - 1, 0, BLK, [(BLK, 1, False)], False)
    attend(0, QH - 1, 1, BLK, [(BLK, 2, False)], True)
    return_keys(1)

    stores = store_queries(1)

    def earlier_own(h, _):
        own(0, h)
        return 0

    lax.fori_loop(0, QH, earlier_own, 0)
    stores += store_queries(0)

    for i in range(BPD):
        r = pl.ds(i * BLK, BLK)
        dkv_copies[i].wait_recv()
        mine = acc[pl.ds(ROWS + i * BLK, BLK), :] * scaled
        dkv_out[r, :] = (mine + dkv_in[r, :].astype(F32)).astype(BF16)
        c = pltpu.make_async_copy(dkv_out.at[r], dkv_ref.at[r], out_sem.at[4 + i])
        c.start()
        stores.append(c)

    kv_copy.wait_send()
    for c in stat_copies:
        c.wait_send()
    for j in range(NCH):
        for side in range(2):
            row_copy(j, side).wait_send()
    for c in dkv_copies:
        c.wait_send()
    for c in stores:
        c.wait()


def place(dq_in, dkv_in, dq_ref, dkv_ref, dq_v, dkv_v, sem_in, sem_out):
    steps = []
    for i in range(PARTS):
        r = pl.ds(i * (ROWS // PARTS), ROWS // PARTS)
        for k, (src, mid, dst) in enumerate(((dq_in, dq_v, dq_ref), (dkv_in, dkv_v, dkv_ref))):
            steps.append(
                (
                    pltpu.make_async_copy(src.at[r], mid.at[r], sem_in.at[2 * i + k]),
                    pltpu.make_async_copy(mid.at[r], dst.at[r], sem_out.at[2 * i + k]),
                )
            )
    for into, _ in steps:
        into.start()
    for into, out in steps:
        into.wait()
        out.start()
    for _, out in steps:
        out.wait()


def on_device(n, queries, outputs, out_grads, log_sums, key_values, holding, block_mask):
    hbm = pl.BlockSpec(memory_space=pltpu.HBM)
    smem = pl.BlockSpec(memory_space=pltpu.SMEM)
    vm = pltpu.VMEM
    dq, dkv = pl.pallas_call(
        functools.partial(kernel, n),
        out_shape=(
            jax.ShapeDtypeStruct((ROWS, QH * HD), BF16),
            jax.ShapeDtypeStruct((ROWS, 2 * HD), BF16),
        ),
        in_specs=[hbm] * 5 + [smem] * 2,
        out_specs=(pl.BlockSpec(memory_space=pl.ANY),) * 2,
        scratch_shapes=[
            vm((2, ROWS, 128), BF16),
            vm((2, ROWS, 128), BF16),
            vm((2, ROWS, 128), BF16),
            vm((QH, ROWS), F32),
            vm((2 * ROWS, 128), BF16),
            vm((HD, 2 * ROWS), BF16),
            vm((BPD, NCH, HALF, 128), BF16),
            vm((2, NCH, HALF, 128), BF16),
            vm((2, NCH, HALF, 128), BF16),
            vm((2, 8, BLK), F32),
            vm((4, 8, BLK), F32),
            vm((BPD, SPAN, 2, QH, 1, HALF), F32),
            vm((BPD, 2, QH, 1, HALF), F32),
            vm((NCH, BPD, 2, HALF, 128), BF16),
            vm((2 * ROWS, 128), F32),
            vm((2, BPD, QH * HD, HALF), F32),
            vm((ROWS, QH * HD), BF16),
            vm((ROWS, 128), BF16),
            vm((ROWS, 128), BF16),
            vm((ROWS, 128), BF16),
            pltpu.SemaphoreType.DMA((8,)),
            pltpu.SemaphoreType.DMA((6,)),
            pltpu.SemaphoreType.DMA((21,)),
            pltpu.SemaphoreType.DMA((21,)),
        ],
        compiler_params=pltpu.CompilerParams(
            collective_id=0, has_side_effects=True, vmem_limit_bytes=60 * 1024 * 1024
        ),
    )(queries, outputs, out_grads, log_sums, key_values, holding, block_mask)
    return pl.pallas_call(
        place,
        out_shape=(
            jax.ShapeDtypeStruct((ROWS, QH * HD), BF16),
            jax.ShapeDtypeStruct((ROWS, 2 * HD), BF16),
        ),
        in_specs=[hbm] * 2,
        out_specs=(pl.BlockSpec(memory_space=pl.ANY),) * 2,
        scratch_shapes=[
            vm((ROWS, QH * HD), BF16),
            vm((ROWS, 2 * HD), BF16),
            pltpu.SemaphoreType.DMA((2 * PARTS,)),
            pltpu.SemaphoreType.DMA((2 * PARTS,)),
        ],
        compiler_params=pltpu.CompilerParams(vmem_limit_bytes=60 * 1024 * 1024),
    )(dq, dkv)


def solution(mesh):
    in_specs = (
        P("blk", "head"),
        P("blk", "head"),
        P("blk", "head"),
        P("head", "blk"),
        P("blk", "head"),
        P(),
        P("blk", None),
    )
    out_specs = (P("blk", "head"), P("blk", "head"))
    return jax.shard_map(
        functools.partial(on_device, mesh.shape["blk"]),
        mesh=mesh, in_specs=in_specs, out_specs=out_specs, check_vma=False,
    )
```

```python
import functools

import jax
import jax.numpy as jnp
from jax import lax
from jax.experimental import pallas as pl
from jax.experimental.pallas import tpu as pltpu
from jax.sharding import PartitionSpec as P

HD = 64
QH = 4
BLK = 512
BPD = 2
SPAN = 3
ROWS = BPD * BLK
HALF = 256
NCH = 8
LOG2E = 1.4426950408889634
SCALE = HD**-0.5
DEAD = 1e30
MESH = pl.DeviceIdType.MESH
F32 = jnp.float32
BF16 = jnp.bfloat16


def nt(a, b):
    return lax.dot_general(a, b, (((1,), (1,)), ((), ())), preferred_element_type=F32)


def nn(a, b):
    return lax.dot_general(a, b, (((1,), (0,)), ((), ())), preferred_element_type=F32)


def pick(cond, a, b):
    return lax.select(jnp.broadcast_to(cond, a.shape), a, b)


class Copy:
    def __init__(self, src, dst, sent, landed, to_next, nxt, prv, has_nxt, has_prv):
        self.args = dict(
            src_ref=src, dst_ref=dst, send_sem=sent, recv_sem=landed,
            device_id={"blk": nxt if to_next else prv}, device_id_type=MESH,
        )
        self.sends, self.receives = (has_nxt, has_prv) if to_next else (has_prv, has_nxt)

    def start(self):
        pl.when(self.sends)(lambda: pltpu.make_async_remote_copy(**self.args).start())

    def wait_send(self):
        pl.when(self.sends)(lambda: pltpu.make_async_remote_copy(**self.args).wait_send())

    def wait_recv(self):
        pl.when(self.receives)(lambda: pltpu.make_async_remote_copy(**self.args).wait_recv())


def kernel(
    n,
    q_ref, o_ref, do_ref, lse_ref, kv_ref, holding_ref, mask_ref,
    dq_ref, own_ref, dkv_in,
    qv, ov, dov, lsev, kvw, ktw, packed, sendb, recvb, stat_send, stat_pool, lsew, deltaw, wbuf,
    acc, dqt, dqo, dkv_send, zeros,
    load_sem, out_sem, send_sem, recv_sem,
):
    me = lax.axis_index("blk")
    nxt = lax.rem(me + 1, n)
    prv = lax.rem(me + n - 1, n)

    has_prv = me > 0
    has_nxt = me < n - 1
    barrier = pltpu.get_barrier_semaphore()

    @pl.when(has_prv)
    def _():
        pl.semaphore_signal(barrier, inc=1, device_id={"blk": prv}, device_id_type=MESH)

    @pl.when(has_nxt)
    def _():
        pl.semaphore_signal(barrier, inc=1, device_id={"blk": nxt}, device_id_type=MESH)

    loads, load_outs = [], []
    for p in range(2):
        cols = pl.ds(p * 128, 128)
        loads.append(pltpu.make_async_copy(q_ref.at[:, cols], qv.at[p], load_sem.at[3 * p]))
        loads.append(pltpu.make_async_copy(do_ref.at[:, cols], dov.at[p], load_sem.at[3 * p + 1]))
        load_outs.append(pltpu.make_async_copy(o_ref.at[:, cols], ov.at[p], load_sem.at[3 * p + 2]))
    load_lse = pltpu.make_async_copy(lse_ref, lsev, load_sem.at[6])
    load_kv = pltpu.make_async_copy(kv_ref, kvw.at[pl.ds(ROWS, ROWS)], load_sem.at[7])
    for c in loads:
        c.start()
    load_kv.start()
    load_lse.start()
    for c in load_outs:
        c.start()

    def remote(src, dst, idx, to_next):
        return Copy(src, dst, send_sem.at[idx], recv_sem.at[idx], to_next, nxt, prv, has_nxt, has_prv)

    kv_copy = remote(kv_ref, kvw.at[pl.ds(0, ROWS)], 0, True)
    stat_copies = [
        remote(stat_send.at[0], stat_pool.at[2], 1, True),
        remote(stat_send.at[1], stat_pool.at[3], 2, False),
    ]
    dkv_copies = [
        remote(dkv_send.at[pl.ds(i * BLK, BLK)], dkv_in.at[pl.ds(i * BLK, BLK)], 3 + i, False)
        for i in range(BPD)
    ]

    def row_copy(j, side):
        return remote(sendb.at[side, j], recvb.at[side, j], 5 + 2 * j + side, side == 0)

    h0 = holding_ref[2 * me]
    h1 = holding_ref[2 * me + 1]
    p0 = holding_ref[2 * prv]
    p1 = holding_ref[2 * prv + 1]
    second = [(h1 >> 1) == me + 1, (h1 >> 1) == me - 1]
    low = lax.broadcasted_iota(jnp.int32, (HALF, 128), 1) < HD

    def send_rows(j):
        row_copy(j, 0).start()
        row_copy(j, 1).start()

    def pack(t, p):
        for slot in range(BPD):
            r = pl.ds(slot * BLK + t * HALF, HALF)
            qf = qv[p, r, :].astype(F32)
            df = dov[p, r, :].astype(F32)
            j = 4 * (1 - t) + 2 * p
            packed[slot, j] = jnp.where(low, qf, pltpu.roll(df, HD, 1)).astype(BF16)
            packed[slot, j + 1] = jnp.where(low, pltpu.roll(qf, HD, 1), df).astype(BF16)
        for j in (j, j + 1):
            for side in range(2):
                sendb[side, j] = pick(second[side], packed[1, j], packed[0, j])


    pl.semaphore_wait(barrier, has_prv.astype(jnp.int32) + has_nxt.astype(jnp.int32))

    kv_copy.start()
    for c in loads[:2]:
        c.wait()
    pack(1, 0)
    for j in range(2):
        for side in range(2):
            row_copy(j, side).start()
    load_kv.wait()

    for c in loads[2:]:
        c.wait()
    load_lse.wait()
    for c in load_outs:
        c.wait()
    head_of = lax.broadcasted_iota(jnp.int32, (8, 128), 1) // HD
    row_of = lax.broadcasted_iota(jnp.int32, (8, 128), 0)
    delta = jnp.zeros((8, ROWS), F32)
    for p in range(2):
        prod = ov[p].astype(F32) * dov[p].astype(F32)
        hi = prod.astype(BF16)
        lo = (prod - hi.astype(F32)).astype(BF16)
        ind = (row_of == head_of + 4 + 2 * p).astype(BF16)
        delta = delta + nt(ind, hi) + nt(ind, lo)
    for slot in range(BPD):
        cols = pl.ds(slot * BLK, BLK)
        stat_pool[slot, 4:8, :] = delta[4:8, slot * BLK : (slot + 1) * BLK]
        stat_pool[slot, 0:4, :] = lsev[:, cols] * LOG2E
    for side in range(2):
        stat_send[side] = pick(second[side], stat_pool[1], stat_pool[0])
        stat_copies[side].start()

    pack(1, 1)
    send_rows(2)
    send_rows(3)
    pack(0, 0)
    send_rows(4)
    send_rows(5)
    pack(0, 1)
    send_rows(6)
    send_rows(7)

    def transpose_keys(base):
        for i in range(ROWS // HALF):
            kt = kvw[pl.ds(base + i * HALF, HALF), :].astype(F32).T
            ktw[:, pl.ds(base + i * HALF, HALF)] = kt[:HD].astype(BF16)

    transpose_keys(ROWS)
    acc[...] = jnp.zeros_like(acc)

    for c in stat_copies:
        c.wait_recv()
    is0, is1, isp = [], [], []
    for s in range(BPD):
        b = BPD * me + s
        is0.append(h0 == b)
        is1.append(h1 == b)
        isp.append((p0 == b) | (p1 == b))

    def choose(s, own0, own1, before, after):
        return pick(is0[s], own0, pick(is1[s], own1, pick(isp[s], before, after)))

    for s in range(BPD):
        st = choose(s, stat_pool[0], stat_pool[1], stat_pool[2], stat_pool[3])
        for w in range(SPAN):
            alive = (mask_ref[s, w] == 1) & (BPD * me + s >= w)
            bias = jnp.where(alive, 0.0, DEAD).astype(F32)
            lw = st + bias
            for h in range(QH):
                for t in range(2):
                    lsew[s, w, t, h] = lw[h : h + 1, t * HALF : (t + 1) * HALF]
        for h in range(QH):
            for t in range(2):
                deltaw[s, t, h] = st[4 + h : 5 + h, t * HALF : (t + 1) * HALF]

    kv_copy.wait_recv()

    @pl.when(me == 0)
    def _():
        kvw[pl.ds(0, ROWS), :] = jnp.zeros((ROWS, 128), BF16)

    @pl.when(me == n - 1)
    def _():
        zeros[...] = jnp.zeros_like(zeros)
        fill = pltpu.make_async_copy(zeros, dkv_in, out_sem.at[5])
        fill.start()
        fill.wait()

    transpose_keys(0)

    causal = lax.broadcasted_iota(jnp.int32, (HALF, HALF), 0) <= lax.broadcasted_iota(
        jnp.int32, (HALF, HALF), 1
    )
    low_half = low[:1].astype(BF16)
    high_half = (~low[:1]).astype(BF16)

    def attend(t, h, s, base, segments, first):
        size = sum(seg[0] for seg in segments)
        rows = pl.ds(base, size)
        j = 4 * (1 - t) + h
        w1 = wbuf[j, s, 0]
        w2 = wbuf[j, s, 1]
        kv = kvw[rows, :]
        scores = nt(kv, w1)
        prob_grads = nt(kv, w2)
        dlt = deltaw[s, t, h]
        probs, grads = [], []
        at = 0
        for count, w, masked in segments:
            pr = jnp.exp2(scores[at : at + count] * (SCALE * LOG2E) - lsew[s, w, t, h])
            if masked:
                pr = jnp.where(causal, pr, 0.0)
            probs.append(pr.astype(BF16))
            grads.append((pr * (prob_grads[at : at + count] - dlt)).astype(BF16))
            at += count
        pb = jnp.concatenate(probs, axis=0) if len(probs) > 1 else probs[0]
        gb = jnp.concatenate(grads, axis=0) if len(grads) > 1 else grads[0]
        acc[rows, :] += nn(gb, w1) + nn(pb, w2)
        part = nn(ktw[:, rows], gb)
        cols = pl.ds(h * HD if isinstance(h, int) else pl.multiple_of(h * HD, HD), HD)
        if first:
            dqt[t, s, cols, :] = part
        else:
            dqt[t, s, cols, :] += part

    def prior(t, h):
        attend(t, h, 0, 0, [(BLK, 2, False), (BLK, 1, False)], True)
        attend(t, h, 1, BLK, [(BLK, 2, False)], True)

    def own(t, h):
        diagonal = [(HALF, 0, False)] * t + [(HALF, 0, True)]
        attend(t, h, 0, ROWS, diagonal, False)
        attend(t, h, 1, ROWS, [(BLK, 1, False)] + diagonal, False)

    def arrive(j):
        row_copy(j, 0).wait_recv()
        row_copy(j, 1).wait_recv()

    def weights(j):
        for s in range(BPD):
            x = choose(s, packed[0, j], packed[1, j], recvb[0, j], recvb[1, j])
            wbuf[j, s, 0] = x * low_half
            wbuf[j, s, 1] = x * high_half

    def send_rows(j):
        row_copy(j, 0).start()
        row_copy(j, 1).start()

    def store_queries(t):
        copies = []
        for s in range(BPD):
            r = pl.ds(s * BLK + t * HALF, HALF)
            dqo[r, :] = (dqt[t, s].T * SCALE).astype(BF16)
            c = pltpu.make_async_copy(dqo.at[r], dq_ref.at[r], out_sem.at[2 * t + s])
            c.start()
            copies.append(c)
        return copies

    def later_rows(h, _):
        arrive(h)
        weights(h)
        prior(1, h)
        own(1, h)
        return 0

    lax.fori_loop(0, QH, later_rows, 0)

    def earlier_rows(h, _):
        j = h + QH
        arrive(j)

        weights(j)
        prior(0, h)
        return 0

    lax.fori_loop(0, QH - 1, earlier_rows, 0)
    arrive(NCH - 1)
    weights(NCH - 1)
    scaled = jnp.where(low[:1], SCALE, 1.0)

    def return_keys(i):
        r = pl.ds(i * BLK, BLK)
        dkv_send[r, :] = (acc[r, :] * scaled).astype(BF16)
        dkv_copies[i].start()

    attend(0, QH - 1, 0, 0, [(BLK, 2, False)], True)
    return_keys(0)
    attend(0, QH - 1, 0, BLK, [(BLK, 1, False)], False)
    attend(0, QH - 1, 1, BLK, [(BLK, 2, False)], True)
    return_keys(1)

    stores = store_queries(1)

    def earlier_own(h, _):
        own(0, h)
        return 0

    lax.fori_loop(0, QH, earlier_own, 0)
    stores += store_queries(0)
    c = pltpu.make_async_copy(acc.at[pl.ds(ROWS, ROWS)], own_ref, out_sem.at[4])
    c.start()
    stores.append(c)

    for c in dkv_copies:
        c.wait_recv()

    kv_copy.wait_send()
    for c in stat_copies:
        c.wait_send()
    for j in range(NCH):
        for side in range(2):
            row_copy(j, side).wait_send()
    for c in dkv_copies:
        c.wait_send()
    for c in stores:
        c.wait()


def finish(dq_in, own, theirs, dq_ref, dkv_ref, dq_v, own_v, theirs_v, sem_in, sem_out):
    half = [pl.ds(i * BLK, BLK) for i in range(BPD)]
    into = []
    for i, r in enumerate(half):
        for k, (src, dst) in enumerate(((own, own_v), (theirs, theirs_v), (dq_in, dq_v))):
            into.append(pltpu.make_async_copy(src.at[r], dst.at[r], sem_in.at[3 * i + k]))
    for c in into:
        c.start()
    scaled = jnp.where(lax.broadcasted_iota(jnp.int32, (1, 128), 1) < HD, SCALE, 1.0)
    out = []
    for i, r in enumerate(half):
        into[3 * i].wait()
        into[3 * i + 1].wait()
        theirs_v[r, :] = (own_v[r, :] * scaled + theirs_v[r, :].astype(F32)).astype(BF16)
        out.append(pltpu.make_async_copy(theirs_v.at[r], dkv_ref.at[r], sem_out.at[2 * i]))
        out[-1].start()
        into[3 * i + 2].wait()
        out.append(pltpu.make_async_copy(dq_v.at[r], dq_ref.at[r], sem_out.at[2 * i + 1]))
        out[-1].start()
    for c in out:
        c.wait()


def on_device(n, queries, outputs, out_grads, log_sums, key_values, holding, block_mask):
    hbm = pl.BlockSpec(memory_space=pltpu.HBM)
    smem = pl.BlockSpec(memory_space=pltpu.SMEM)
    vm = pltpu.VMEM
    dq, mine, theirs = pl.pallas_call(
        functools.partial(kernel, n),
        out_shape=(
            jax.ShapeDtypeStruct((ROWS, QH * HD), BF16),
            jax.ShapeDtypeStruct((ROWS, 2 * HD), F32),
            jax.ShapeDtypeStruct((ROWS, 2 * HD), BF16),
        ),
        in_specs=[hbm] * 5 + [smem] * 2,
        out_specs=(pl.BlockSpec(memory_space=pl.ANY),) * 3,
        scratch_shapes=[
            vm((2, ROWS, 128), BF16),
            vm((2, ROWS, 128), BF16),
            vm((2, ROWS, 128), BF16),
            vm((QH, ROWS), F32),
            vm((2 * ROWS, 128), BF16),
            vm((HD, 2 * ROWS), BF16),
            vm((BPD, NCH, HALF, 128), BF16),
            vm((2, NCH, HALF, 128), BF16),
            vm((2, NCH, HALF, 128), BF16),
            vm((2, 8, BLK), F32),
            vm((4, 8, BLK), F32),
            vm((BPD, SPAN, 2, QH, 1, HALF), F32),
            vm((BPD, 2, QH, 1, HALF), F32),
            vm((NCH, BPD, 2, HALF, 128), BF16),
            vm((2 * ROWS, 128), F32),
            vm((2, BPD, QH * HD, HALF), F32),
            vm((ROWS, QH * HD), BF16),
            vm((ROWS, 128), BF16),
            vm((ROWS, 128), BF16),
            pltpu.SemaphoreType.DMA((8,)),
            pltpu.SemaphoreType.DMA((6,)),
            pltpu.SemaphoreType.DMA((21,)),
            pltpu.SemaphoreType.DMA((21,)),
        ],
        compiler_params=pltpu.CompilerParams(
            collective_id=0, has_side_effects=True, vmem_limit_bytes=60 * 1024 * 1024
        ),
    )(queries, outputs, out_grads, log_sums, key_values, holding, block_mask)
    return pl.pallas_call(
        finish,
        out_shape=(
            jax.ShapeDtypeStruct((ROWS, QH * HD), BF16),
            jax.ShapeDtypeStruct((ROWS, 2 * HD), BF16),
        ),
        in_specs=[hbm] * 3,
        out_specs=(pl.BlockSpec(memory_space=pl.ANY),) * 2,
        scratch_shapes=[
            vm((ROWS, QH * HD), BF16),
            vm((ROWS, 2 * HD), F32),
            vm((ROWS, 2 * HD), BF16),
            pltpu.SemaphoreType.DMA((6,)),
            pltpu.SemaphoreType.DMA((4,)),
        ],
        compiler_params=pltpu.CompilerParams(vmem_limit_bytes=60 * 1024 * 1024),
    )(dq, mine, theirs)


def solution(mesh):
    in_specs = (
        P("blk", "head"),
        P("blk", "head"),
        P("blk", "head"),
        P("head", "blk"),
        P("blk", "head"),
        P(),
        P("blk", None),
    )
    out_specs = (P("blk", "head"), P("blk", "head"))
    return jax.shard_map(
        functools.partial(on_device, mesh.shape["blk"]),
        mesh=mesh, in_specs=in_specs, out_specs=out_specs, check_vma=False,
    )
```

```python
import functools

import jax
import jax.numpy as jnp
from jax import lax
from jax.experimental import pallas as pl
from jax.experimental.pallas import tpu as pltpu
from jax.sharding import PartitionSpec as P

HD = 64
QH = 4
BLK = 512
BPD = 2
SPAN = 3
ROWS = BPD * BLK
HALF = 256
NCH = 8
LOG2E = 1.4426950408889634
SCALE = HD**-0.5
DEAD = 1e30
MESH = pl.DeviceIdType.MESH
F32 = jnp.float32
BF16 = jnp.bfloat16


def nt(a, b):
    return lax.dot_general(a, b, (((1,), (1,)), ((), ())), preferred_element_type=F32)


def nn(a, b):
    return lax.dot_general(a, b, (((1,), (0,)), ((), ())), preferred_element_type=F32)


def pick(cond, a, b):
    return lax.select(jnp.broadcast_to(cond, a.shape), a, b)


class Copy:
    def __init__(self, src, dst, sent, landed, to_next, nxt, prv, has_nxt, has_prv):
        self.args = dict(
            src_ref=src, dst_ref=dst, send_sem=sent, recv_sem=landed,
            device_id={"blk": nxt if to_next else prv}, device_id_type=MESH,
        )
        self.sends, self.receives = (has_nxt, has_prv) if to_next else (has_prv, has_nxt)

    def start(self):
        pl.when(self.sends)(lambda: pltpu.make_async_remote_copy(**self.args).start())

    def wait_send(self):
        pl.when(self.sends)(lambda: pltpu.make_async_remote_copy(**self.args).wait_send())

    def wait_recv(self):
        pl.when(self.receives)(lambda: pltpu.make_async_remote_copy(**self.args).wait_recv())


def kernel(
    n,
    q_ref, o_ref, do_ref, lse_ref, kv_ref, holding_hbm, mask_hbm,
    dq_ref, own_ref, dkv_in,
    qv, ov, dov, lsev, kvw, ktw, packed, sendb, recvb, stat_send, stat_pool, lsew, deltaw, wbuf,
    acc, dqt, dkv_send, holding_ref, mask_ref,

    load_sem, send_sem, recv_sem,
):
    me = lax.axis_index("blk")
    nxt = lax.rem(me + 1, n)
    prv = lax.rem(me + n - 1, n)

    has_prv = me > 0
    has_nxt = me < n - 1
    barrier = pltpu.get_barrier_semaphore()

    @pl.when(has_prv)
    def _():
        pl.semaphore_signal(barrier, inc=1, device_id={"blk": prv}, device_id_type=MESH)

    @pl.when(has_nxt)
    def _():
        pl.semaphore_signal(barrier, inc=1, device_id={"blk": nxt}, device_id_type=MESH)

    loads, load_outs = [], []
    for p in range(2):
        cols = pl.ds(p * 128, 128)
        loads.append(pltpu.make_async_copy(q_ref.at[:, cols], qv.at[p], load_sem.at[3 * p]))
        loads.append(pltpu.make_async_copy(do_ref.at[:, cols], dov.at[p], load_sem.at[3 * p + 1]))
        load_outs.append(pltpu.make_async_copy(o_ref.at[:, cols], ov.at[p], load_sem.at[3 * p + 2]))
    load_lse = pltpu.make_async_copy(lse_ref, lsev, load_sem.at[6])
    load_kv = pltpu.make_async_copy(kv_ref, kvw.at[pl.ds(ROWS, ROWS)], load_sem.at[7])
    small = [
        pltpu.make_async_copy(holding_hbm, holding_ref, load_sem.at[8]),
        pltpu.make_async_copy(mask_hbm, mask_ref, load_sem.at[9]),
    ]
    for c in small + loads:
        c.start()
    load_kv.start()
    load_lse.start()
    for c in load_outs:
        c.start()

    def remote(src, dst, idx, to_next):
        return Copy(src, dst, send_sem.at[idx], recv_sem.at[idx], to_next, nxt, prv, has_nxt, has_prv)

    kv_copy = remote(kv_ref, kvw.at[pl.ds(0, ROWS)], 0, True)
    stat_copies = [
        remote(stat_send.at[0], stat_pool.at[2], 1, True),
        remote(stat_send.at[1], stat_pool.at[3], 2, False),
    ]
    dkv_copies = [
        remote(dkv_send.at[pl.ds(i * BLK, BLK)], dkv_in.at[pl.ds(i * BLK, BLK)], 3 + i, False)
        for i in range(BPD)
    ]

    def row_copy(j, side):
        return remote(sendb.at[side, j], recvb.at[side, j], 5 + 2 * j + side, side == 0)

    low = lax.broadcasted_iota(jnp.int32, (HALF, 128), 1) < HD

    def send_rows(j):
        row_copy(j, 0).start()
        row_copy(j, 1).start()

    def pack(t, p):
        for slot in range(BPD):
            r = pl.ds(slot * BLK + t * HALF, HALF)
            qf = qv[p, r, :].astype(F32)
            df = dov[p, r, :].astype(F32)
            j = 4 * (1 - t) + 2 * p
            packed[slot, j] = jnp.where(low, qf, pltpu.roll(df, HD, 1)).astype(BF16)
            packed[slot, j + 1] = jnp.where(low, pltpu.roll(qf, HD, 1), df).astype(BF16)
        for j in (j, j + 1):
            for side in range(2):
                sendb[side, j] = pick(second[side], packed[1, j], packed[0, j])


    pl.semaphore_wait(barrier, has_prv.astype(jnp.int32) + has_nxt.astype(jnp.int32))

    kv_copy.start()
    for c in small:
        c.wait()
    h0 = holding_ref[2 * me]
    h1 = holding_ref[2 * me + 1]
    p0 = holding_ref[2 * prv]
    p1 = holding_ref[2 * prv + 1]
    second = [(h1 >> 1) == me + 1, (h1 >> 1) == me - 1]
    for c in loads[:2]:
        c.wait()
    pack(1, 0)
    for j in range(2):
        for side in range(2):
            row_copy(j, side).start()
    load_kv.wait()

    for c in loads[2:]:
        c.wait()
    load_lse.wait()
    for c in load_outs:
        c.wait()
    head_of = lax.broadcasted_iota(jnp.int32, (8, 128), 1) // HD
    row_of = lax.broadcasted_iota(jnp.int32, (8, 128), 0)
    delta = jnp.zeros((8, ROWS), F32)
    for p in range(2):
        prod = ov[p].astype(F32) * dov[p].astype(F32)
        hi = prod.astype(BF16)
        lo = (prod - hi.astype(F32)).astype(BF16)
        ind = (row_of == head_of + 4 + 2 * p).astype(BF16)
        delta = delta + nt(ind, hi) + nt(ind, lo)
    for slot in range(BPD):
        cols = pl.ds(slot * BLK, BLK)
        stat_pool[slot, 4:8, :] = delta[4:8, slot * BLK : (slot + 1) * BLK]
        stat_pool[slot, 0:4, :] = lsev[:, cols] * LOG2E
    for side in range(2):
        stat_send[side] = pick(second[side], stat_pool[1], stat_pool[0])
        stat_copies[side].start()

    pack(1, 1)
    send_rows(2)
    send_rows(3)
    pack(0, 0)
    send_rows(4)
    send_rows(5)
    pack(0, 1)
    send_rows(6)
    send_rows(7)

    def transpose_keys(base):
        for i in range(ROWS // HALF):
            kt = kvw[pl.ds(base + i * HALF, HALF), :].astype(F32).T
            ktw[:, pl.ds(base + i * HALF, HALF)] = kt[:HD].astype(BF16)

    transpose_keys(ROWS)
    acc[...] = jnp.zeros_like(acc)

    for c in stat_copies:
        c.wait_recv()
    is0, is1, isp = [], [], []
    for s in range(BPD):
        b = BPD * me + s
        is0.append(h0 == b)
        is1.append(h1 == b)
        isp.append((p0 == b) | (p1 == b))

    def choose(s, own0, own1, before, after):
        return pick(is0[s], own0, pick(is1[s], own1, pick(isp[s], before, after)))

    for s in range(BPD):
        st = choose(s, stat_pool[0], stat_pool[1], stat_pool[2], stat_pool[3])
        for w in range(SPAN):
            alive = (mask_ref[s, w] == 1) & (BPD * me + s >= w)
            bias = jnp.where(alive, 0.0, DEAD).astype(F32)
            lw = st + bias
            for h in range(QH):
                for t in range(2):
                    lsew[s, w, t, h] = lw[h : h + 1, t * HALF : (t + 1) * HALF]
        for h in range(QH):
            for t in range(2):
                deltaw[s, t, h] = st[4 + h : 5 + h, t * HALF : (t + 1) * HALF]

    kv_copy.wait_recv()

    @pl.when(me == 0)
    def _():
        kvw[pl.ds(0, ROWS), :] = jnp.zeros((ROWS, 128), BF16)

    @pl.when(me == n - 1)
    def _():
        dkv_in[...] = jnp.zeros_like(dkv_in)

    transpose_keys(0)

    causal = lax.broadcasted_iota(jnp.int32, (HALF, HALF), 0) <= lax.broadcasted_iota(
        jnp.int32, (HALF, HALF), 1
    )
    low_half = low[:1].astype(BF16)
    high_half = (~low[:1]).astype(BF16)

    def attend(t, h, s, base, segments, first):
        size = sum(seg[0] for seg in segments)
        rows = pl.ds(base, size)
        j = 4 * (1 - t) + h
        w1 = wbuf[j, s, 0]
        w2 = wbuf[j, s, 1]
        kv = kvw[rows, :]
        scores = nt(kv, w1)
        prob_grads = nt(kv, w2)
        dlt = deltaw[s, t, h]
        probs, grads = [], []
        at = 0
        for count, w, masked in segments:
            pr = jnp.exp2(scores[at : at + count] * (SCALE * LOG2E) - lsew[s, w, t, h])
            if masked:
                pr = jnp.where(causal, pr, 0.0)
            probs.append(pr.astype(BF16))
            grads.append((pr * (prob_grads[at : at + count] - dlt)).astype(BF16))
            at += count
        pb = jnp.concatenate(probs, axis=0) if len(probs) > 1 else probs[0]
        gb = jnp.concatenate(grads, axis=0) if len(grads) > 1 else grads[0]
        acc[rows, :] += nn(gb, w1) + nn(pb, w2)
        part = nn(ktw[:, rows], gb)
        cols = pl.ds(h * HD if isinstance(h, int) else pl.multiple_of(h * HD, HD), HD)
        if first:
            dqt[t, s, cols, :] = part
        else:
            dqt[t, s, cols, :] += part

    def prior(t, h):
        attend(t, h, 0, 0, [(BLK, 2, False), (BLK, 1, False)], True)
        attend(t, h, 1, BLK, [(BLK, 2, False)], True)

    def own(t, h):
        diagonal = [(HALF, 0, False)] * t + [(HALF, 0, True)]
        attend(t, h, 0, ROWS, diagonal, False)
        attend(t, h, 1, ROWS, [(BLK, 1, False)] + diagonal, False)

    def arrive(j):
        row_copy(j, 0).wait_recv()
        row_copy(j, 1).wait_recv()

    def weights(j):
        for s in range(BPD):
            x = choose(s, packed[0, j], packed[1, j], recvb[0, j], recvb[1, j])
            wbuf[j, s, 0] = x * low_half
            wbuf[j, s, 1] = x * high_half

    def send_rows(j):
        row_copy(j, 0).start()
        row_copy(j, 1).start()

    def store_queries(t):
        for s in range(BPD):
            r = pl.ds(s * BLK + t * HALF, HALF)
            dq_ref[r, :] = (dqt[t, s].T * SCALE).astype(BF16)

    def later_rows(h, _):
        arrive(h)
        weights(h)
        prior(1, h)
        own(1, h)
        return 0

    lax.fori_loop(0, QH, later_rows, 0)

    def earlier_rows(h, _):
        j = h + QH
        arrive(j)

        weights(j)
        prior(0, h)
        return 0

    lax.fori_loop(0, QH - 1, earlier_rows, 0)
    arrive(NCH - 1)
    weights(NCH - 1)
    scaled = jnp.where(low[:1], SCALE, 1.0)

    def return_keys(i):
        r = pl.ds(i * BLK, BLK)
        dkv_send[r, :] = (acc[r, :] * scaled).astype(BF16)
        dkv_copies[i].start()

    attend(0, QH - 1, 0, 0, [(BLK, 2, False)], True)
    return_keys(0)
    attend(0, QH - 1, 0, BLK, [(BLK, 1, False)], False)
    attend(0, QH - 1, 1, BLK, [(BLK, 2, False)], True)
    return_keys(1)

    store_queries(1)

    def earlier_own(h, _):
        own(0, h)
        return 0

    lax.fori_loop(0, QH, earlier_own, 0)
    store_queries(0)
    own_ref[...] = acc[pl.ds(ROWS, ROWS), :] * scaled

    for c in dkv_copies:
        c.wait_recv()

    kv_copy.wait_send()
    for c in stat_copies:
        c.wait_send()
    for j in range(NCH):
        for side in range(2):
            row_copy(j, side).wait_send()
    for c in dkv_copies:
        c.wait_send()


def finish(dq_in, own, theirs, dq_ref, dkv_ref, total, sem):
    out = [pltpu.make_async_copy(dq_in, dq_ref, sem.at[0])]
    out[0].start()
    for i in range(BPD):
        r = pl.ds(i * BLK, BLK)
        total[r, :] = (own[r, :] + theirs[r, :].astype(F32)).astype(BF16)
        out.append(pltpu.make_async_copy(total.at[r], dkv_ref.at[r], sem.at[1 + i]))
        out[-1].start()
    for c in out:
        c.wait()


def on_device(n, queries, outputs, out_grads, log_sums, key_values, holding, block_mask):
    hbm = pl.BlockSpec(memory_space=pltpu.HBM)
    vm = pltpu.VMEM
    dq, mine, theirs = pl.pallas_call(
        functools.partial(kernel, n),
        out_shape=(
            vm((ROWS, QH * HD), BF16),
            vm((ROWS, 2 * HD), F32),
            vm((ROWS, 2 * HD), BF16),
        ),
        in_specs=[hbm] * 7,
        out_specs=(pl.BlockSpec(memory_space=pltpu.VMEM),) * 3,
        scratch_shapes=[
            vm((2, ROWS, 128), BF16),
            vm((2, ROWS, 128), BF16),
            vm((2, ROWS, 128), BF16),
            vm((QH, ROWS), F32),
            vm((2 * ROWS, 128), BF16),
            vm((HD, 2 * ROWS), BF16),
            vm((BPD, NCH, HALF, 128), BF16),
            vm((2, NCH, HALF, 128), BF16),
            vm((2, NCH, HALF, 128), BF16),
            vm((2, 8, BLK), F32),
            vm((4, 8, BLK), F32),
            vm((BPD, SPAN, 2, QH, 1, HALF), F32),
            vm((BPD, 2, QH, 1, HALF), F32),
            vm((NCH, BPD, 2, HALF, 128), BF16),
            vm((2 * ROWS, 128), F32),
            vm((2, BPD, QH * HD, HALF), F32),
            vm((ROWS, 128), BF16),
            pltpu.SMEM((holding.shape[0],), jnp.int32),
            pltpu.SMEM((BPD, SPAN), jnp.int32),
            pltpu.SemaphoreType.DMA((10,)),
            pltpu.SemaphoreType.DMA((21,)),
            pltpu.SemaphoreType.DMA((21,)),
        ],
        compiler_params=pltpu.CompilerParams(
            collective_id=0, has_side_effects=True, vmem_limit_bytes=40 * 1024 * 1024
        ),
    )(
        *(
            pltpu.with_memory_space_constraint(x, pltpu.HBM)
            for x in (queries, outputs, out_grads, log_sums, key_values, holding, block_mask)
        )
    )
    return pl.pallas_call(
        finish,
        out_shape=(
            jax.ShapeDtypeStruct((ROWS, QH * HD), BF16),
            jax.ShapeDtypeStruct((ROWS, 2 * HD), BF16),
        ),
        in_specs=[pl.BlockSpec(memory_space=pltpu.VMEM)] * 3,
        out_specs=(pl.BlockSpec(memory_space=pl.ANY),) * 2,
        scratch_shapes=[vm((ROWS, 2 * HD), BF16), pltpu.SemaphoreType.DMA((1 + BPD,))],
        compiler_params=pltpu.CompilerParams(vmem_limit_bytes=40 * 1024 * 1024),
    )(*(pltpu.with_memory_space_constraint(x, pltpu.VMEM) for x in (dq, mine, theirs)))


def solution(mesh):
    in_specs = (
        P("blk", "head"),
        P("blk", "head"),
        P("blk", "head"),
        P("head", "blk"),
        P("blk", "head"),
        P(),
        P("blk", None),
    )
    out_specs = (P("blk", "head"), P("blk", "head"))
    return jax.shard_map(
        functools.partial(on_device, mesh.shape["blk"]),
        mesh=mesh, in_specs=in_specs, out_specs=out_specs, check_vma=False,
    )
```

```python
import functools

import jax
import jax.numpy as jnp
from jax import lax
from jax.experimental import pallas as pl
from jax.experimental.pallas import tpu as pltpu
from jax.sharding import PartitionSpec as P

HD = 64
QH = 4
BLK = 512
BPD = 2
SPAN = 3
ROWS = BPD * BLK
HALF = 256
NCH = 8
LOG2E = 1.4426950408889634
SCALE = HD**-0.5
DEAD = 1e30
MESH = pl.DeviceIdType.MESH
F32 = jnp.float32
BF16 = jnp.bfloat16


def nt(a, b):
    return lax.dot_general(a, b, (((1,), (1,)), ((), ())), preferred_element_type=F32)


def nn(a, b):
    return lax.dot_general(a, b, (((1,), (0,)), ((), ())), preferred_element_type=F32)


def pick(cond, a, b):
    return lax.select(jnp.broadcast_to(cond, a.shape), a, b)


class Copy:
    def __init__(self, src, dst, sent, landed, to_next, nxt, prv, has_nxt, has_prv):
        self.args = dict(
            src_ref=src, dst_ref=dst, send_sem=sent, recv_sem=landed,
            device_id={"blk": nxt if to_next else prv}, device_id_type=MESH,
        )
        self.sends, self.receives = (has_nxt, has_prv) if to_next else (has_prv, has_nxt)

    def start(self):
        pl.when(self.sends)(lambda: pltpu.make_async_remote_copy(**self.args).start())

    def wait_send(self):
        pl.when(self.sends)(lambda: pltpu.make_async_remote_copy(**self.args).wait_send())

    def wait_recv(self):
        pl.when(self.receives)(lambda: pltpu.make_async_remote_copy(**self.args).wait_recv())


def kernel(
    n,
    q_ref, o_ref, do_ref, lse_ref, kv_ref, holding_hbm, mask_hbm,
    dq_ref, own_ref, dkv_in,
    qv, ov, dov, lsev, kvw, ktw, packed, sendb, recvb, stat_send, stat_pool, lsew, deltaw, wbuf,
    acc, dqt, dkv_send, holding_ref, mask_ref,

    load_sem, send_sem, recv_sem,
):
    me = lax.axis_index("blk")
    nxt = lax.rem(me + 1, n)
    prv = lax.rem(me + n - 1, n)

    has_prv = me > 0
    has_nxt = me < n - 1
    barrier = pltpu.get_barrier_semaphore()

    @pl.when(has_prv)
    def _():
        pl.semaphore_signal(barrier, inc=1, device_id={"blk": prv}, device_id_type=MESH)

    @pl.when(has_nxt)
    def _():
        pl.semaphore_signal(barrier, inc=1, device_id={"blk": nxt}, device_id_type=MESH)

    loads, load_outs = [], []
    for p in range(2):
        cols = pl.ds(p * 128, 128)
        loads.append(pltpu.make_async_copy(q_ref.at[:, cols], qv.at[p], load_sem.at[3 * p]))
        loads.append(pltpu.make_async_copy(do_ref.at[:, cols], dov.at[p], load_sem.at[3 * p + 1]))
        load_outs.append(pltpu.make_async_copy(o_ref.at[:, cols], ov.at[p], load_sem.at[3 * p + 2]))
    load_lse = pltpu.make_async_copy(lse_ref, lsev, load_sem.at[6])
    load_kv = pltpu.make_async_copy(kv_ref, kvw.at[pl.ds(ROWS, ROWS)], load_sem.at[7])
    small = [
        pltpu.make_async_copy(holding_hbm, holding_ref, load_sem.at[8]),
        pltpu.make_async_copy(mask_hbm, mask_ref, load_sem.at[9]),
    ]
    for c in small + loads:
        c.start()
    load_kv.start()
    load_lse.start()
    for c in load_outs:
        c.start()

    def remote(src, dst, idx, to_next):
        return Copy(src, dst, send_sem.at[idx], recv_sem.at[idx], to_next, nxt, prv, has_nxt, has_prv)

    kv_copy = remote(kv_ref, kvw.at[pl.ds(0, ROWS)], 0, True)
    stat_copies = [
        remote(stat_send.at[0], stat_pool.at[2], 1, True),
        remote(stat_send.at[1], stat_pool.at[3], 2, False),
    ]
    dkv_copies = [
        remote(dkv_send.at[pl.ds(i * BLK, BLK)], dkv_in.at[pl.ds(i * BLK, BLK)], 3 + i, False)
        for i in range(BPD)
    ]

    def row_copy(j, side):
        return remote(sendb.at[side, j], recvb.at[side, j], 5 + 2 * j + side, side == 0)

    low = lax.broadcasted_iota(jnp.int32, (HALF, 128), 1) < HD

    def send_rows(j):
        row_copy(j, 0).start()
        row_copy(j, 1).start()

    def pack(t, p):
        for slot in range(BPD):
            r = pl.ds(slot * BLK + t * HALF, HALF)
            qf = qv[p, r, :].astype(F32)
            df = dov[p, r, :].astype(F32)
            j = 4 * (1 - t) + 2 * p
            packed[slot, j] = jnp.where(low, qf, pltpu.roll(df, HD, 1)).astype(BF16)
            packed[slot, j + 1] = jnp.where(low, pltpu.roll(qf, HD, 1), df).astype(BF16)
        for j in (j, j + 1):
            for side in range(2):
                sendb[side, j] = pick(second[side], packed[1, j], packed[0, j])


    pl.semaphore_wait(barrier, has_prv.astype(jnp.int32) + has_nxt.astype(jnp.int32))

    kv_copy.start()
    for c in small:
        c.wait()
    h0 = holding_ref[2 * me]
    h1 = holding_ref[2 * me + 1]
    p0 = holding_ref[2 * prv]
    p1 = holding_ref[2 * prv + 1]
    second = [(h1 >> 1) == me + 1, (h1 >> 1) == me - 1]
    for c in loads[:2]:
        c.wait()
    pack(1, 0)
    for j in range(2):
        for side in range(2):
            row_copy(j, side).start()
    load_kv.wait()

    for c in loads[2:]:
        c.wait()
    load_lse.wait()
    for c in load_outs:
        c.wait()
    head_of = lax.broadcasted_iota(jnp.int32, (8, 128), 1) // HD
    row_of = lax.broadcasted_iota(jnp.int32, (8, 128), 0)
    delta = jnp.zeros((8, ROWS), F32)
    for p in range(2):
        prod = ov[p].astype(F32) * dov[p].astype(F32)
        hi = prod.astype(BF16)
        lo = (prod - hi.astype(F32)).astype(BF16)
        ind = (row_of == head_of + 4 + 2 * p).astype(BF16)
        delta = delta + nt(ind, hi) + nt(ind, lo)
    for slot in range(BPD):
        cols = pl.ds(slot * BLK, BLK)
        stat_pool[slot, 4:8, :] = delta[4:8, slot * BLK : (slot + 1) * BLK]
        stat_pool[slot, 0:4, :] = lsev[:, cols] * LOG2E
    for side in range(2):
        stat_send[side] = pick(second[side], stat_pool[1], stat_pool[0])
        stat_copies[side].start()

    pack(1, 1)
    send_rows(2)
    send_rows(3)
    pack(0, 0)
    send_rows(4)
    send_rows(5)
    pack(0, 1)
    send_rows(6)
    send_rows(7)

    def transpose_keys(base):
        for i in range(ROWS // HALF):
            kt = kvw[pl.ds(base + i * HALF, HALF), :].astype(F32).T
            ktw[:, pl.ds(base + i * HALF, HALF)] = kt[:HD].astype(BF16)

    transpose_keys(ROWS)
    acc[...] = jnp.zeros_like(acc)

    for c in stat_copies:
        c.wait_recv()
    is0, is1, isp = [], [], []
    for s in range(BPD):
        b = BPD * me + s
        is0.append(h0 == b)
        is1.append(h1 == b)
        isp.append((p0 == b) | (p1 == b))

    def choose(s, own0, own1, before, after):
        return pick(is0[s], own0, pick(is1[s], own1, pick(isp[s], before, after)))

    for s in range(BPD):
        st = choose(s, stat_pool[0], stat_pool[1], stat_pool[2], stat_pool[3])
        for w in range(SPAN):
            alive = (mask_ref[s, w] == 1) & (BPD * me + s >= w)
            bias = jnp.where(alive, 0.0, DEAD).astype(F32)
            lw = st + bias
            for h in range(QH):
                for t in range(2):
                    lsew[s, w, t, h] = lw[h : h + 1, t * HALF : (t + 1) * HALF]
        for h in range(QH):
            for t in range(2):
                deltaw[s, t, h] = st[4 + h : 5 + h, t * HALF : (t + 1) * HALF]

    kv_copy.wait_recv()

    @pl.when(me == 0)
    def _():
        kvw[pl.ds(0, ROWS), :] = jnp.zeros((ROWS, 128), BF16)

    @pl.when(me == n - 1)
    def _():
        dkv_in[...] = jnp.zeros_like(dkv_in)

    transpose_keys(0)

    causal = lax.broadcasted_iota(jnp.int32, (HALF, HALF), 0) <= lax.broadcasted_iota(
        jnp.int32, (HALF, HALF), 1
    )
    low_half = low[:1].astype(BF16)
    high_half = (~low[:1]).astype(BF16)

    def attend(t, h, s, base, segments, first):
        size = sum(seg[0] for seg in segments)
        rows = pl.ds(base, size)
        j = 4 * (1 - t) + h
        w1 = wbuf[j, s, 0]
        w2 = wbuf[j, s, 1]
        kv = kvw[rows, :]
        scores = nt(kv, w1)
        prob_grads = nt(kv, w2)
        dlt = deltaw[s, t, h]
        probs, grads = [], []
        at = 0
        for count, w, masked in segments:
            pr = jnp.exp2(scores[at : at + count] * (SCALE * LOG2E) - lsew[s, w, t, h])
            if masked:
                pr = jnp.where(causal, pr, 0.0)
            probs.append(pr.astype(BF16))
            grads.append((pr * (prob_grads[at : at + count] - dlt)).astype(BF16))
            at += count
        pb = jnp.concatenate(probs, axis=0) if len(probs) > 1 else probs[0]
        gb = jnp.concatenate(grads, axis=0) if len(grads) > 1 else grads[0]
        acc[rows, :] += nn(gb, w1) + nn(pb, w2)
        part = nn(ktw[:, rows], gb)
        cols = pl.ds(h * HD if isinstance(h, int) else pl.multiple_of(h * HD, HD), HD)
        if first:
            dqt[t, s, cols, :] = part
        else:
            dqt[t, s, cols, :] += part

    def prior(t, h):
        attend(t, h, 0, 0, [(BLK, 2, False), (BLK, 1, False)], True)
        attend(t, h, 1, BLK, [(BLK, 2, False)], True)

    def own(t, h):
        diagonal = [(HALF, 0, False)] * t + [(HALF, 0, True)]
        attend(t, h, 0, ROWS, diagonal, False)
        attend(t, h, 1, ROWS, [(BLK, 1, False)] + diagonal, False)

    def arrive(j):
        row_copy(j, 0).wait_recv()
        row_copy(j, 1).wait_recv()

    def weights(j):
        for s in range(BPD):
            x = choose(s, packed[0, j], packed[1, j], recvb[0, j], recvb[1, j])
            wbuf[j, s, 0] = x * low_half
            wbuf[j, s, 1] = x * high_half

    def send_rows(j):
        row_copy(j, 0).start()
        row_copy(j, 1).start()

    def store_queries(t):
        for s in range(BPD):
            r = pl.ds(s * BLK + t * HALF, HALF)
            dq_ref[r, :] = (dqt[t, s].T * SCALE).astype(BF16)

    def later_rows(h, _):
        arrive(h)
        weights(h)
        prior(1, h)
        own(1, h)
        return 0

    lax.fori_loop(0, QH, later_rows, 0)

    def earlier_rows(h, _):
        j = h + QH
        arrive(j)

        weights(j)
        prior(0, h)
        return 0

    lax.fori_loop(0, QH - 1, earlier_rows, 0)
    arrive(NCH - 1)
    weights(NCH - 1)
    scaled = jnp.where(low[:1], SCALE, 1.0)

    def return_keys(i):
        r = pl.ds(i * BLK, BLK)
        dkv_send[r, :] = (acc[r, :] * scaled).astype(BF16)
        dkv_copies[i].start()

    attend(0, QH - 1, 0, 0, [(BLK, 2, False)], True)
    return_keys(0)
    attend(0, QH - 1, 0, BLK, [(BLK, 1, False)], False)
    attend(0, QH - 1, 1, BLK, [(BLK, 2, False)], True)
    return_keys(1)

    store_queries(1)

    def earlier_own(h, _):
        own(0, h)
        return 0

    lax.fori_loop(0, QH, earlier_own, 0)
    store_queries(0)
    own_ref[...] = acc[pl.ds(ROWS, ROWS), :] * scaled

    kv_copy.wait_send()
    for c in stat_copies:
        c.wait_send()
    for j in range(NCH):
        for side in range(2):
            row_copy(j, side).wait_send()
    for c in dkv_copies:
        c.wait_send()
    for c in dkv_copies:
        c.wait_recv()


def finish(dq_in, own, theirs, dq_ref, dkv_ref, total, sem):
    out = [pltpu.make_async_copy(dq_in, dq_ref, sem.at[0])]
    out[0].start()
    for i in range(BPD):
        r = pl.ds(i * BLK, BLK)
        total[r, :] = (own[r, :] + theirs[r, :].astype(F32)).astype(BF16)
        out.append(pltpu.make_async_copy(total.at[r], dkv_ref.at[r], sem.at[1 + i]))
        out[-1].start()
    for c in out:
        c.wait()


def on_device(n, queries, outputs, out_grads, log_sums, key_values, holding, block_mask):
    hbm = pl.BlockSpec(memory_space=pltpu.HBM)
    vm = pltpu.VMEM
    dq, mine, theirs = pl.pallas_call(
        functools.partial(kernel, n),
        out_shape=(
            vm((ROWS, QH * HD), BF16),
            vm((ROWS, 2 * HD), F32),
            vm((ROWS, 2 * HD), BF16),
        ),
        in_specs=[hbm] * 7,
        out_specs=(pl.BlockSpec(memory_space=pltpu.VMEM),) * 3,
        scratch_shapes=[
            vm((2, ROWS, 128), BF16),
            vm((2, ROWS, 128), BF16),
            vm((2, ROWS, 128), BF16),
            vm((QH, ROWS), F32),
            vm((2 * ROWS, 128), BF16),
            vm((HD, 2 * ROWS), BF16),
            vm((BPD, NCH, HALF, 128), BF16),
            vm((2, NCH, HALF, 128), BF16),
            vm((2, NCH, HALF, 128), BF16),
            vm((2, 8, BLK), F32),
            vm((4, 8, BLK), F32),
            vm((BPD, SPAN, 2, QH, 1, HALF), F32),
            vm((BPD, 2, QH, 1, HALF), F32),
            vm((NCH, BPD, 2, HALF, 128), BF16),
            vm((2 * ROWS, 128), F32),
            vm((2, BPD, QH * HD, HALF), F32),
            vm((ROWS, 128), BF16),
            pltpu.SMEM((holding.shape[0],), jnp.int32),
            pltpu.SMEM((BPD, SPAN), jnp.int32),
            pltpu.SemaphoreType.DMA((10,)),
            pltpu.SemaphoreType.DMA((21,)),
            pltpu.SemaphoreType.DMA((21,)),
        ],
        compiler_params=pltpu.CompilerParams(
            collective_id=0, has_side_effects=True, vmem_limit_bytes=40 * 1024 * 1024
        ),
    )(
        *(
            pltpu.with_memory_space_constraint(x, pltpu.HBM)
            for x in (queries, outputs, out_grads, log_sums, key_values, holding, block_mask)
        )
    )
    return pl.pallas_call(
        finish,
        out_shape=(
            jax.ShapeDtypeStruct((ROWS, QH * HD), BF16),
            jax.ShapeDtypeStruct((ROWS, 2 * HD), BF16),
        ),
        in_specs=[pl.BlockSpec(memory_space=pltpu.VMEM)] * 3,
        out_specs=(pl.BlockSpec(memory_space=pl.ANY),) * 2,
        scratch_shapes=[vm((ROWS, 2 * HD), BF16), pltpu.SemaphoreType.DMA((1 + BPD,))],
        compiler_params=pltpu.CompilerParams(vmem_limit_bytes=40 * 1024 * 1024),
    )(*(pltpu.with_memory_space_constraint(x, pltpu.VMEM) for x in (dq, mine, theirs)))


def solution(mesh):
    in_specs = (
        P("blk", "head"),
        P("blk", "head"),
        P("blk", "head"),
        P("head", "blk"),
        P("blk", "head"),
        P(),
        P("blk", None),
    )
    out_specs = (P("blk", "head"), P("blk", "head"))
    return jax.shard_map(
        functools.partial(on_device, mesh.shape["blk"]),
        mesh=mesh, in_specs=in_specs, out_specs=out_specs, check_vma=False,
    )
```

```python
import functools

import jax
import jax.numpy as jnp
from jax import lax
from jax.experimental import pallas as pl
from jax.experimental.pallas import tpu as pltpu
from jax.sharding import PartitionSpec as P

HD = 64
QH = 4
BLK = 512
BPD = 2
SPAN = 3
ROWS = BPD * BLK
HALF = 256
NCH = 8
LOG2E = 1.4426950408889634
SCALE = HD**-0.5
DEAD = 1e30
MESH = pl.DeviceIdType.MESH
F32 = jnp.float32
BF16 = jnp.bfloat16


def nt(a, b):
    return lax.dot_general(a, b, (((1,), (1,)), ((), ())), preferred_element_type=F32)


def nn(a, b):
    return lax.dot_general(a, b, (((1,), (0,)), ((), ())), preferred_element_type=F32)


def pick(cond, a, b):
    return lax.select(jnp.broadcast_to(cond, a.shape), a, b)


class Copy:
    def __init__(self, src, dst, sent, landed, to_next, nxt, prv, has_nxt, has_prv):
        self.args = dict(
            src_ref=src, dst_ref=dst, send_sem=sent, recv_sem=landed,
            device_id={"blk": nxt if to_next else prv}, device_id_type=MESH,
        )
        self.sends, self.receives = (has_nxt, has_prv) if to_next else (has_prv, has_nxt)

    def start(self):
        pl.when(self.sends)(lambda: pltpu.make_async_remote_copy(**self.args).start())

    def wait_send(self):
        pl.when(self.sends)(lambda: pltpu.make_async_remote_copy(**self.args).wait_send())

    def wait_recv(self):
        pl.when(self.receives)(lambda: pltpu.make_async_remote_copy(**self.args).wait_recv())


def kernel(
    n,
    q_ref, o_ref, do_ref, lse_ref, kv_ref, holding_hbm, mask_hbm,
    dq_ref, own_ref, dkv_in,
    qv, ov, dov, lsev, kvw, ktw, packed, sendb, recvb, stat_send, stat_pool, lsew, deltaw, wbuf,
    acc, dqt, dkv_send, holding_ref, mask_ref,

    load_sem, send_sem, recv_sem,
):
    me = lax.axis_index("blk")
    nxt = lax.rem(me + 1, n)
    prv = lax.rem(me + n - 1, n)

    has_prv = me > 0
    has_nxt = me < n - 1
    barrier = pltpu.get_barrier_semaphore()

    @pl.when(has_prv)
    def _():
        pl.semaphore_signal(barrier, inc=1, device_id={"blk": prv}, device_id_type=MESH)

    @pl.when(has_nxt)
    def _():
        pl.semaphore_signal(barrier, inc=1, device_id={"blk": nxt}, device_id_type=MESH)

    loads, load_outs = [], []
    for p in range(2):
        cols = pl.ds(p * 128, 128)
        loads.append(pltpu.make_async_copy(q_ref.at[:, cols], qv.at[p], load_sem.at[3 * p]))
        loads.append(pltpu.make_async_copy(do_ref.at[:, cols], dov.at[p], load_sem.at[3 * p + 1]))
        load_outs.append(pltpu.make_async_copy(o_ref.at[:, cols], ov.at[p], load_sem.at[3 * p + 2]))
    load_lse = pltpu.make_async_copy(lse_ref, lsev, load_sem.at[6])
    load_kv = pltpu.make_async_copy(kv_ref, kvw.at[pl.ds(ROWS, ROWS)], load_sem.at[7])
    small = [
        pltpu.make_async_copy(holding_hbm, holding_ref, load_sem.at[8]),
        pltpu.make_async_copy(mask_hbm, mask_ref, load_sem.at[9]),
    ]
    for c in small + loads:
        c.start()
    load_kv.start()
    load_lse.start()
    for c in load_outs:
        c.start()

    def remote(src, dst, idx, to_next):
        return Copy(src, dst, send_sem.at[idx], recv_sem.at[idx], to_next, nxt, prv, has_nxt, has_prv)

    kv_copy = remote(kv_ref, kvw.at[pl.ds(0, ROWS)], 0, True)
    stat_copies = [
        remote(stat_send.at[0], stat_pool.at[2], 1, True),
        remote(stat_send.at[1], stat_pool.at[3], 2, False),
    ]
    dkv_copies = [
        remote(dkv_send.at[pl.ds(i * BLK, BLK)], dkv_in.at[pl.ds(i * BLK, BLK)], 3 + i, False)
        for i in range(BPD)
    ]

    def row_copy(j, side):
        return remote(sendb.at[side, j], recvb.at[side, j], 5 + 2 * j + side, side == 0)

    low = lax.broadcasted_iota(jnp.int32, (HALF, 128), 1) < HD

    def send_rows(j):
        row_copy(j, 0).start()
        row_copy(j, 1).start()

    def pack(t, p):
        for slot in range(BPD):
            r = pl.ds(slot * BLK + t * HALF, HALF)
            qf = qv[p, r, :].astype(F32)
            df = dov[p, r, :].astype(F32)
            j = 4 * (1 - t) + 2 * p
            packed[slot, j] = jnp.where(low, qf, pltpu.roll(df, HD, 1)).astype(BF16)
            packed[slot, j + 1] = jnp.where(low, pltpu.roll(qf, HD, 1), df).astype(BF16)
        for j in (j, j + 1):
            for side in range(2):
                sendb[side, j] = pick(second[side], packed[1, j], packed[0, j])


    pl.semaphore_wait(barrier, has_prv.astype(jnp.int32) + has_nxt.astype(jnp.int32))

    kv_copy.start()
    for c in small:
        c.wait()
    h0 = holding_ref[2 * me]
    h1 = holding_ref[2 * me + 1]
    p0 = holding_ref[2 * prv]
    p1 = holding_ref[2 * prv + 1]
    second = [(h1 >> 1) == me + 1, (h1 >> 1) == me - 1]
    for c in loads[:2]:
        c.wait()
    pack(1, 0)
    for j in range(2):
        for side in range(2):
            row_copy(j, side).start()
    load_kv.wait()

    for c in loads[2:]:
        c.wait()
    load_lse.wait()
    for c in load_outs:
        c.wait()
    head_of = lax.broadcasted_iota(jnp.int32, (8, 128), 1) // HD
    row_of = lax.broadcasted_iota(jnp.int32, (8, 128), 0)
    delta = jnp.zeros((8, ROWS), F32)
    for p in range(2):
        prod = ov[p].astype(F32) * dov[p].astype(F32)
        hi = prod.astype(BF16)
        lo = (prod - hi.astype(F32)).astype(BF16)
        ind = (row_of == head_of + 4 + 2 * p).astype(BF16)
        delta = delta + nt(ind, hi) + nt(ind, lo)
    for slot in range(BPD):
        cols = pl.ds(slot * BLK, BLK)
        stat_pool[slot, 4:8, :] = delta[4:8, slot * BLK : (slot + 1) * BLK]
        stat_pool[slot, 0:4, :] = lsev[:, cols] * LOG2E
    for side in range(2):
        stat_send[side] = pick(second[side], stat_pool[1], stat_pool[0])
        stat_copies[side].start()

    pack(1, 1)
    send_rows(2)
    send_rows(3)
    pack(0, 0)
    send_rows(4)
    send_rows(5)
    pack(0, 1)
    send_rows(6)
    send_rows(7)

    def transpose_keys(base):
        for i in range(ROWS // HALF):
            kt = kvw[pl.ds(base + i * HALF, HALF), :].astype(F32).T
            ktw[:, pl.ds(base + i * HALF, HALF)] = kt[:HD].astype(BF16)

    transpose_keys(ROWS)
    acc[...] = jnp.zeros_like(acc)

    for c in stat_copies:
        c.wait_recv()
    is0, is1, isp = [], [], []
    for s in range(BPD):
        b = BPD * me + s
        is0.append(h0 == b)
        is1.append(h1 == b)
        isp.append((p0 == b) | (p1 == b))

    def choose(s, own0, own1, before, after):
        return pick(is0[s], own0, pick(is1[s], own1, pick(isp[s], before, after)))

    for s in range(BPD):
        st = choose(s, stat_pool[0], stat_pool[1], stat_pool[2], stat_pool[3])
        for w in range(SPAN):
            alive = (mask_ref[s, w] == 1) & (BPD * me + s >= w)
            bias = jnp.where(alive, 0.0, DEAD).astype(F32)
            lw = st + bias
            for h in range(QH):
                for t in range(2):
                    lsew[s, w, t, h] = lw[h : h + 1, t * HALF : (t + 1) * HALF]
        for h in range(QH):
            for t in range(2):
                deltaw[s, t, h] = st[4 + h : 5 + h, t * HALF : (t + 1) * HALF]

    kv_copy.wait_recv()

    @pl.when(me == 0)
    def _():
        kvw[pl.ds(0, ROWS), :] = jnp.zeros((ROWS, 128), BF16)

    @pl.when(me == n - 1)
    def _():
        dkv_in[...] = jnp.zeros_like(dkv_in)

    transpose_keys(0)

    causal = lax.broadcasted_iota(jnp.int32, (HALF, HALF), 0) <= lax.broadcasted_iota(
        jnp.int32, (HALF, HALF), 1
    )
    low_half = low[:1].astype(BF16)
    high_half = (~low[:1]).astype(BF16)

    def attend(t, h, s, base, segments, first):
        size = sum(seg[0] for seg in segments)
        rows = pl.ds(base, size)
        j = 4 * (1 - t) + h
        w1 = wbuf[j, s, 0]
        w2 = wbuf[j, s, 1]
        kv = kvw[rows, :]
        scores = nt(kv, w1)
        prob_grads = nt(kv, w2)
        dlt = deltaw[s, t, h]
        probs, grads = [], []
        at = 0
        for count, w, masked in segments:
            pr = jnp.exp2(scores[at : at + count] * (SCALE * LOG2E) - lsew[s, w, t, h])
            if masked:
                pr = jnp.where(causal, pr, 0.0)
            probs.append(pr.astype(BF16))
            grads.append((pr * (prob_grads[at : at + count] - dlt)).astype(BF16))
            at += count
        pb = jnp.concatenate(probs, axis=0) if len(probs) > 1 else probs[0]
        gb = jnp.concatenate(grads, axis=0) if len(grads) > 1 else grads[0]
        acc[rows, :] += nn(gb, w1) + nn(pb, w2)
        part = nn(ktw[:, rows], gb)
        cols = pl.ds(h * HD if isinstance(h, int) else pl.multiple_of(h * HD, HD), HD)
        if first:
            dqt[t, s, cols, :] = part
        else:
            dqt[t, s, cols, :] += part

    def prior(t, h):
        attend(t, h, 0, 0, [(BLK, 2, False), (BLK, 1, False)], True)
        attend(t, h, 1, BLK, [(BLK, 2, False)], True)

    def own(t, h):
        diagonal = [(HALF, 0, False)] * t + [(HALF, 0, True)]
        attend(t, h, 0, ROWS, diagonal, False)
        attend(t, h, 1, ROWS, [(BLK, 1, False)] + diagonal, False)

    def arrive(j):
        row_copy(j, 0).wait_recv()
        row_copy(j, 1).wait_recv()

    def weights(j):
        for s in range(BPD):
            x = choose(s, packed[0, j], packed[1, j], recvb[0, j], recvb[1, j])
            wbuf[j, s, 0] = x * low_half
            wbuf[j, s, 1] = x * high_half

    def send_rows(j):
        row_copy(j, 0).start()
        row_copy(j, 1).start()

    def store_queries(t):
        for s in range(BPD):
            r = pl.ds(s * BLK + t * HALF, HALF)
            dq_ref[r, :] = (dqt[t, s].T * SCALE).astype(BF16)

    def later_rows(h, _):
        arrive(h)
        weights(h)
        prior(1, h)
        own(1, h)
        return 0

    lax.fori_loop(0, QH, later_rows, 0)

    def earlier_rows(h, _):
        j = h + QH
        arrive(j)

        weights(j)
        prior(0, h)
        return 0

    lax.fori_loop(0, QH - 2, earlier_rows, 0)
    scaled = jnp.where(low[:1], SCALE, 1.0)

    def return_keys(i):
        r = pl.ds(i * BLK, BLK)
        dkv_send[r, :] = (acc[r, :] * scaled).astype(BF16)
        dkv_copies[i].start()

    for h in (QH - 2, QH - 1):
        arrive(QH + h)
        weights(QH + h)
        attend(0, h, 0, 0, [(BLK, 2, False)], True)
    return_keys(0)
    for h in (QH - 2, QH - 1):
        attend(0, h, 0, BLK, [(BLK, 1, False)], False)
        attend(0, h, 1, BLK, [(BLK, 2, False)], True)
    return_keys(1)

    store_queries(1)

    def earlier_own(h, _):
        own(0, h)
        return 0

    lax.fori_loop(0, QH, earlier_own, 0)
    store_queries(0)
    own_ref[...] = acc[pl.ds(ROWS, ROWS), :] * scaled

    kv_copy.wait_send()
    for c in stat_copies:
        c.wait_send()
    for j in range(NCH):
        for side in range(2):
            row_copy(j, side).wait_send()
    for c in dkv_copies:
        c.wait_send()
    for c in dkv_copies:
        c.wait_recv()


def finish(dq_in, own, theirs, dq_ref, dkv_ref, total, sem):
    out = [pltpu.make_async_copy(dq_in, dq_ref, sem.at[0])]
    out[0].start()
    for i in range(BPD):
        r = pl.ds(i * BLK, BLK)
        total[r, :] = (own[r, :] + theirs[r, :].astype(F32)).astype(BF16)
        out.append(pltpu.make_async_copy(total.at[r], dkv_ref.at[r], sem.at[1 + i]))
        out[-1].start()
    for c in out:
        c.wait()


def on_device(n, queries, outputs, out_grads, log_sums, key_values, holding, block_mask):
    hbm = pl.BlockSpec(memory_space=pltpu.HBM)
    vm = pltpu.VMEM
    dq, mine, theirs = pl.pallas_call(
        functools.partial(kernel, n),
        out_shape=(
            vm((ROWS, QH * HD), BF16),
            vm((ROWS, 2 * HD), F32),
            vm((ROWS, 2 * HD), BF16),
        ),
        in_specs=[hbm] * 7,
        out_specs=(pl.BlockSpec(memory_space=pltpu.VMEM),) * 3,
        scratch_shapes=[
            vm((2, ROWS, 128), BF16),
            vm((2, ROWS, 128), BF16),
            vm((2, ROWS, 128), BF16),
            vm((QH, ROWS), F32),
            vm((2 * ROWS, 128), BF16),
            vm((HD, 2 * ROWS), BF16),
            vm((BPD, NCH, HALF, 128), BF16),
            vm((2, NCH, HALF, 128), BF16),
            vm((2, NCH, HALF, 128), BF16),
            vm((2, 8, BLK), F32),
            vm((4, 8, BLK), F32),
            vm((BPD, SPAN, 2, QH, 1, HALF), F32),
            vm((BPD, 2, QH, 1, HALF), F32),
            vm((NCH, BPD, 2, HALF, 128), BF16),
            vm((2 * ROWS, 128), F32),
            vm((2, BPD, QH * HD, HALF), F32),
            vm((ROWS, 128), BF16),
            pltpu.SMEM((holding.shape[0],), jnp.int32),
            pltpu.SMEM((BPD, SPAN), jnp.int32),
            pltpu.SemaphoreType.DMA((10,)),
            pltpu.SemaphoreType.DMA((21,)),
            pltpu.SemaphoreType.DMA((21,)),
        ],
        compiler_params=pltpu.CompilerParams(
            collective_id=0, has_side_effects=True, vmem_limit_bytes=40 * 1024 * 1024
        ),
    )(
        *(
            pltpu.with_memory_space_constraint(x, pltpu.HBM)
            for x in (queries, outputs, out_grads, log_sums, key_values, holding, block_mask)
        )
    )
    return pl.pallas_call(
        finish,
        out_shape=(
            jax.ShapeDtypeStruct((ROWS, QH * HD), BF16),
            jax.ShapeDtypeStruct((ROWS, 2 * HD), BF16),
        ),
        in_specs=[pl.BlockSpec(memory_space=pltpu.VMEM)] * 3,
        out_specs=(pl.BlockSpec(memory_space=pl.ANY),) * 2,
        scratch_shapes=[vm((ROWS, 2 * HD), BF16), pltpu.SemaphoreType.DMA((1 + BPD,))],
        compiler_params=pltpu.CompilerParams(vmem_limit_bytes=40 * 1024 * 1024),
    )(*(pltpu.with_memory_space_constraint(x, pltpu.VMEM) for x in (dq, mine, theirs)))


def solution(mesh):
    in_specs = (
        P("blk", "head"),
        P("blk", "head"),
        P("blk", "head"),
        P("head", "blk"),
        P("blk", "head"),
        P(),
        P("blk", None),
    )
    out_specs = (P("blk", "head"), P("blk", "head"))
    return jax.shard_map(
        functools.partial(on_device, mesh.shape["blk"]),
        mesh=mesh, in_specs=in_specs, out_specs=out_specs, check_vma=False,
    )
```
